128 devices in a mesh: dp: 16 (over x, y), tensor: 8 (over z, core).
Axes of the slice: x: 4, y: 4, z: 4, core: 2. Of those that a mesh axis runs over, the one named last changes fastest.
Arguments:
- gate_pre: bfloat16 [8192, 14336], P('dp', 'tensor'), may hold values from -6 to 6
- up_pre: bfloat16 [8192, 14336], P('dp', 'tensor'), may hold values from -6 to 6
- down_weight: bfloat16 [14336, 4096], P('tensor', 'dp'), as said below
- grad_out: bfloat16 [8192, 4096], P('dp', 'tensor'), may hold values from -6 to 6
- weight_history: float32 [16], replicated
- act_history: float32 [16], replicated
Outputs:
- mixed: bfloat16 [8192, 4096], P('dp', 'tensor')
- grad_gate: bfloat16 [8192, 14336], P('dp', 'tensor')
- grad_up: bfloat16 [8192, 14336], P('dp', 'tensor')
- weight_grad: bfloat16 [14336, 4096], P('tensor', 'dp')
- new_weight_history: float32 [16], replicated
- new_act_history: float32 [16], replicated
The draws below stay inside these ranges and needn't reach their ends.
Inputs may be any that keep to these rules, and one draw needn't show every extreme that they name: Entries of down_weight lie within 24 / sqrt(14336) in magnitude.
All inputs are finite; a program needn't handle non-finite values.
Results may differ from the reference program's by a relative error of at most 0.019.
Values may be sent and summed in bfloat16 or wider, within the bound.
No kernel may reach another device: no remote copies, remote signals or barrier semaphores. Data moves between devices by JAX's collectives and lax.ppermute only.
A program may use at most 192 MiB of HBM per device.

```python
import math
import jax
import jax.numpy as jnp
from jax import lax

D = 4096
FF = 14336
TOK_DEV = 512
HIST = 16
TOKENS = 8192
N_DP = 16


def draw_down_weight(key, part):
    key = jax.random.fold_in(key, 11)
    key_rows, key_cols, key_base = jax.random.split(key, 3)
    row_scale = jnp.exp(jax.random.uniform(key_rows, (FF, 1), jnp.float32) * math.log(10.0))
    col_scale = jnp.exp(jax.random.uniform(key_cols, (1, D), jnp.float32) * math.log(10.0))
    base = jnp.clip(jax.random.normal(key_base, (FF, D), jnp.float32), -5.0, 5.0)
    return (base * row_scale * col_scale / (21.5 * math.sqrt(FF))).astype(jnp.bfloat16)


def draw_weight_history(key, part):
    key = jax.random.fold_in(key, 12)
    values = jax.random.uniform(key, (HIST,), jnp.float32, 1.5, 5.0)
    return values / math.sqrt(FF)


def draw_act_history(key, part):
    key = jax.random.fold_in(key, 13)
    return jax.random.uniform(key, (HIST,), jnp.float32, 0.75, 3.0)


def with_spikes(entries, own_key, source, target, blocks, factor):
    def block_of(position):
        return (jnp.arange(entries.shape[position]) // (entries.shape[position] // blocks)).reshape((-1,) + (1,) * (entries.ndim - 1 - position))

    one_side = jax.random.permutation(own_key, blocks)[block_of(target)]
    far = (block_of(target) + blocks // 2) % blocks
    return jnp.where((block_of(source) == one_side) | (block_of(source) == far), factor * entries, entries)


def block_levels(stream_key, extent, pieces, low, high):
    def one(position, shards_of):
        draws = jax.random.uniform(jax.random.fold_in(jax.random.fold_in(stream_key, 6), position), (shards_of,), jnp.float32, low / len(pieces), high / len(pieces))
        return jnp.repeat(jnp.exp(draws), extent[position] // shards_of).reshape((-1,) + (1,) * (len(extent) - position - 1))

    level = one(*pieces[0])
    for cut in pieces[1:]:
        level = level * one(*cut)
    return level


def bell_draw(stream_key, dims, scale, bound, pieces=(), dtype=jnp.bfloat16):
    drawn = scale * jax.random.normal(stream_key, dims, jnp.float32)
    if pieces:
        drawn = drawn * block_levels(stream_key, dims, pieces, -0.22, 0.18)
    return jnp.clip(drawn, -bound, bound).astype(dtype)


def heavy_noise(own_key, dims, scale, bound, cuts, heavy, dtype=jnp.bfloat16):
    values = scale * jax.random.normal(own_key, dims, jnp.float32)
    if cuts:
        values = values * block_levels(own_key, dims, cuts, -0.22, 0.18)
    return jnp.clip(with_spikes(values, jax.random.fold_in(own_key, 3), *heavy), -bound, bound).astype(dtype)


def setup_inputs(seed: int = 0) -> dict:
    keys = jax.random.split(jax.random.key(seed), 7)
    gate_pre = bell_draw(keys[0], (TOKENS, FF), 1.0, 6.0, ((0, 16), (1, 8)))
    up_pre = bell_draw(keys[1], (TOKENS, FF), 1.0, 6.0, ((0, 16), (1, 8)))
    down_weight = draw_down_weight(jax.random.fold_in(keys[6], 71), 0)
    grad_out = heavy_noise(keys[3], (TOKENS, D), 1.0, 6.0, ((0, 16), (1, 8)), (0, 1, 16, 2.0))
    weight_history = draw_weight_history(jax.random.fold_in(keys[6], 71), 0)
    act_history = draw_act_history(jax.random.fold_in(keys[6], 71), 0)
    return dict(gate_pre=gate_pre, up_pre=up_pre, down_weight=down_weight, grad_out=grad_out, weight_history=weight_history, act_history=act_history)


def reference(gate_pre, up_pre, down_weight, grad_out, weight_history, act_history):
    gate = gate_pre.astype(jnp.float32)
    up = up_pre.astype(jnp.float32)
    sigm = jax.nn.sigmoid(gate)
    silu_gate = gate * sigm
    act = silu_gate * up
    act_limit = jnp.max(act_history)
    act_q = jnp.clip(act, -act_limit, act_limit).astype(jnp.bfloat16)
    weight_limit = jnp.max(weight_history)
    weight_full = down_weight.astype(jnp.float32)
    weight_q = jnp.clip(weight_full, -weight_limit, weight_limit).astype(jnp.bfloat16)
    mixed = jnp.dot(act_q, weight_q, preferred_element_type=jnp.float32).astype(jnp.bfloat16)
    grad_act = jnp.dot(grad_out, weight_q.T, preferred_element_type=jnp.float32)
    grad_gate = (grad_act * up * sigm * (1.0 + gate * (1.0 - sigm))).astype(jnp.bfloat16)
    grad_up = (grad_act * silu_gate).astype(jnp.bfloat16)
    act_groups = act_q.reshape(N_DP, TOK_DEV, FF)
    grad_groups = grad_out.reshape(N_DP, TOK_DEV, D)

    def add_group(total, pair):
        part_sum = jnp.dot(pair[0].T, pair[1], preferred_element_type=jnp.float32).astype(jnp.bfloat16)
        part_sum = lax.optimization_barrier(part_sum)
        return total + part_sum.astype(jnp.float32), None

    total, _ = lax.scan(add_group, jnp.zeros((FF, D), jnp.float32), (act_groups, grad_groups))
    weight_grad = total.astype(jnp.bfloat16)
    weight_peak = jnp.max(jnp.abs(weight_full))
    act_peak = jnp.max(jnp.abs(act))
    new_weight_history = jnp.concatenate([weight_peak[None], weight_history[:-1]])
    new_act_history = jnp.concatenate([act_peak[None], act_history[:-1]])
    return mixed, grad_gate, grad_up, weight_grad, new_weight_history, new_act_history
```

```python
import functools

import jax
import jax.numpy as jnp
import numpy as np
from jax import lax
from jax.experimental import pallas as pl
from jax.experimental.pallas import tpu as pltpu
from jax.sharding import Mesh, PartitionSpec as P

AXES = ("x", "y", "z", "c")
N = 4
BF16 = jnp.bfloat16
F32 = jnp.float32
VMEM_BYTES = 24 * 1024 * 1024
ANYWHERE = pl.BlockSpec(memory_space=pl.ANY)
SCALARS = pl.BlockSpec(memory_space=pltpu.SMEM)
IN_VMEM = pl.BlockSpec(memory_space=pltpu.VMEM)
IN_HBM = pl.BlockSpec(memory_space=pltpu.HBM)
NOTE = 16


def flat(x, y, z, c):
    return ((x % N * N + y % N) * N + z % N) * 2 + c


def places():
    return [(x, y, z, c) for x in range(N) for y in range(N) for z in range(N) for c in range(2)]


def token_ring(step):
    return [
        (flat(x, y, z, c), flat(x, y + step, z, c) if c == 0 else flat(x + step, y, z, c))
        for x, y, z, c in places()
    ]


def feature_ring(step):
    return [
        (flat(x, y, z, c), flat(x + step, y, z, c) if c == 0 else flat(x, y + step, z, c))
        for x, y, z, c in places()
    ]


def hidden_ring(step):
    return [(flat(x, y, z, c), flat(x, y, z + step, c)) for x, y, z, c in places()]


def token_groups():
    first = [[flat(x, y, z, 0) for y in range(N)] for x in range(N) for z in range(N)]
    second = [[flat(x, y, z, 1) for x in range(N)] for y in range(N) for z in range(N)]
    return first + second


def tile_edges():
    edges = []
    for x, y, z, c in places():
        for half in range(2):
            block = 2 * c + half
            edges.append((flat(x, y, z, c), flat(x, block, z, 0), half, y))
            edges.append((flat(x, y, z, c), flat(z, y, block, 1), half, x))
    return edges


def rounds():
    rest = tile_edges()
    out = []
    for _ in range(4):
        outgoing = {}
        for edge in rest:
            outgoing.setdefault(edge[0], []).append(edge)
        chosen = {}

        def augment(owner, seen):
            for edge in outgoing[owner]:
                if edge[1] in seen:
                    continue
                seen.add(edge[1])
                if edge[1] not in chosen or augment(chosen[edge[1]][0], seen):
                    chosen[edge[1]] = edge
                    return True
            return False

        for owner in range(128):
            augment(owner, set())
        picked = sorted(chosen.values())
        out.append(picked)
        rest = [edge for edge in rest if edge not in picked]
    return out


ROUNDS = rounds()
TABLE = np.zeros((8, 128), np.int32)
for number, picked in enumerate(ROUNDS):
    for owner, user, half, slot in picked:
        TABLE[number, owner] = half
        TABLE[4 + number, user] = slot


def send(value, pairs):
    return lax.ppermute(value, AXES, pairs)


def here():
    x, y, z, c = (lax.axis_index(name) for name in AXES)
    return flat(x, y, z, c), jnp.where(c == 0, x, y), z


def call(kernel, out_shape, cost, in_specs, operands, after=(), stored=(), vmem=VMEM_BYTES, **options):
    flops, moved = cost
    count = len(operands)
    extra = len(after) + len(stored)

    def body(*refs):
        kernel(*refs[:count], *refs[count + extra :])

    return pl.pallas_call(
        body,
        out_shape=out_shape,
        in_specs=list(in_specs) + [ANYWHERE] * len(after) + [IN_HBM] * len(stored),
        compiler_params=pltpu.CompilerParams(vmem_limit_bytes=vmem),
        cost_estimate=pl.CostEstimate(flops=flops, bytes_accessed=moved, transcendentals=0),
        **options,
    )(*operands, *after, *stored)


def shape(*dims, dtype=BF16):
    return jax.ShapeDtypeStruct(dims, dtype)


def ring_gather(own, ring):
    far = send(own, ring(2))
    return own, send(own, ring(-1)), far, send(own, ring(1))


def ring_exchange(parts, ring):
    far = send(parts[2], ring(2))
    return parts[0], send(parts[1], ring(1)), far, send(parts[3], ring(-1))


def peak_of(values):
    return jnp.max(jnp.abs(values), axis=0, keepdims=True)


def keep_peak(step, top, peak):
    @pl.when(step == 0)
    def _():
        top[...] = peak

    @pl.when(step > 0)
    def _():
        top[...] = jnp.maximum(top[...], peak)


def row_blocks(array, steps):
    return pl.BlockSpec((array.shape[0] // steps, array.shape[1]), lambda i: (i, 0))


def fixed(*dims):
    return pl.BlockSpec(dims, lambda i: (0, 0))


def note_of(peaks, width):
    row = lax.broadcasted_iota(jnp.int32, (NOTE, width), 0)
    note = jnp.zeros((NOTE, width), F32)
    for number in range(2):
        rest = jnp.broadcast_to(peaks[number : number + 1, :1], (NOTE, width))
        for piece in range(3):
            value = rest.astype(BF16).astype(F32)
            note = jnp.where(row == 3 * number + piece, value, note)
            rest = rest - value
    return note.astype(BF16)


def peaks_in(notes):
    best = []
    for number in range(2):
        values = []
        for note in notes:
            note = note[...].astype(F32)
            pieces = [note[3 * number + piece : 3 * number + piece + 1, :128] for piece in range(3)]
            values.append(pieces[0] + pieces[1] + pieces[2])
        best.append(functools.reduce(jnp.maximum, values))
    row = lax.broadcasted_iota(jnp.int32, (8, 128), 0)
    return jnp.where(row == 0, jnp.broadcast_to(best[0], (8, 128)), jnp.broadcast_to(best[1], (8, 128)))


def note_block(array):
    last = array.shape[0] // NOTE - 1
    return pl.BlockSpec((NOTE, array.shape[1]), lambda *i: (last, 0))


def share_kernel(table, grad, peaks, others, out0, out1, out2, out3):
    me, _, _ = here()
    tokens, width = grad.shape[0], grad.shape[1] // 2
    note = note_of(jnp.maximum(peaks[...], others[...]), width)
    for number, out in enumerate((out0, out1, out2, out3)):
        half = table[number, me]

        @pl.when(half == 0)
        def _():
            out[:tokens, :] = grad[:, :width]

        @pl.when(half == 1)
        def _():
            out[:tokens, :] = grad[:, width:]

        out[tokens:, :] = note


def share(grad, peaks, others):
    block = shape(grad.shape[0] + NOTE, grad.shape[1] // 2)
    return call(
        share_kernel,
        (block, block, block, block),
        (0, 0),
        [SCALARS] + [IN_VMEM] * 3,
        (jnp.asarray(TABLE), grad, peaks, others),
        out_specs=[IN_VMEM] * 4,
    )


def activate_kernel(gate, up, weight, act_history, weight_history,
                    act_q, weight_q, peaks, act_top, weight_top):
    step = pl.program_id(0)
    gate_v = gate[...].astype(F32)
    act = gate_v * jax.nn.sigmoid(gate_v) * up[...].astype(F32)
    limit = jnp.max(act_history[...], axis=1, keepdims=True)
    act_q[...] = jnp.clip(act, -limit, limit).astype(BF16)
    weight_v = weight[...].astype(F32)
    limit = jnp.max(weight_history[...], axis=1, keepdims=True)
    weight_q[...] = jnp.clip(weight_v, -limit, limit).astype(BF16)
    keep_peak(step, act_top, peak_of(act))
    keep_peak(step, weight_top, peak_of(weight_v))

    @pl.when(step == pl.num_programs(0) - 1)
    def _():
        row = lax.broadcasted_iota(jnp.int32, peaks.shape, 0)
        top = jnp.max(act_top[...], axis=1, keepdims=True)
        other = jnp.max(weight_top[...], axis=1, keepdims=True)
        peaks[...] = jnp.where(
            row == 0, jnp.broadcast_to(top, peaks.shape), jnp.broadcast_to(other, peaks.shape)
        )


def activate(gate, up, weight, act_history, weight_history):
    steps = 8
    rows, weight_rows = row_blocks(gate, steps), row_blocks(weight, steps)
    return call(
        activate_kernel,
        (shape(*gate.shape), shape(*weight.shape), shape(8, 128, dtype=F32)),
        (0, 0),
        [rows, rows, weight_rows, fixed(1, act_history.shape[1]), fixed(1, act_history.shape[1])],
        (gate, up, weight, act_history, weight_history),
        grid=(steps,),
        out_specs=[rows, weight_rows, fixed(8, 128)],
        scratch_shapes=[pltpu.VMEM((1, gate.shape[1]), F32), pltpu.VMEM((1, weight.shape[1]), F32)],
    )


def slopes_kernel(gate, up, slope, silu, token):
    gate_v = gate[...].astype(F32)
    sigm = jax.nn.sigmoid(gate_v)
    slope[...] = (up[...].astype(F32) * sigm * (1.0 + gate_v * (1.0 - sigm))).astype(BF16)
    silu[...] = (gate_v * sigm).astype(BF16)
    token[...] = jnp.zeros(token.shape, F32)


def slopes(gate, up, after):
    steps = 8
    rows = row_blocks(gate, steps)
    return call(
        slopes_kernel,
        (shape(*gate.shape), shape(*gate.shape), shape(8, 128, dtype=F32)),
        (0, 0),
        [rows, rows],
        (gate, up),
        after,
        grid=(steps,),
        out_specs=[rows, rows, fixed(8, 128)],
    )


def place_kernel(table, in0, in1, in2, in3, out):
    me, _, _ = here()
    rows = in0.shape[0] - NOTE
    for number, block in enumerate((in0, in1, in2, in3)):
        start = pl.multiple_of(table[4 + number, me] * rows, rows)
        out[pl.ds(start, rows), :] = block[:rows, :]
    peaks = peaks_in([block[rows:, :] for block in (in0, in1, in2, in3)])
    out[4 * rows :, :] = note_of(peaks, out.shape[1])


def place(blocks):
    rows, features = blocks[0].shape
    return call(
        place_kernel,
        shape(4 * (rows - NOTE) + NOTE, features),
        (0, 0),
        [SCALARS] + [IN_VMEM] * 4,
        (jnp.asarray(TABLE), *blocks),
        out_specs=IN_VMEM,
    )


def gate_kernel(*refs):
    pass


def gate(values, after=(), stored=()):
    count = len(values)
    return call(
        gate_kernel,
        tuple(shape(*value.shape) for value in values),
        (0, 0),
        [ANYWHERE] * count,
        values,
        after,
        stored,
        vmem=1024 * 1024,
        out_specs=[ANYWHERE] * count,
        input_output_aliases={number: number for number in range(count)},
    )


def columns_kernel(place, own, after, far, before, out):
    width = own.shape[1]
    for step, block in enumerate((own, after, far, before)):
        column = pl.multiple_of(lax.rem(place + step, N) * width, width)
        out[:, pl.ds(column, width)] = block[...]


def weight_tile_kernel(*refs):
    columns_kernel(here()[1], *refs)


def weight_tile(parts, after):
    steps = 4
    out = shape(parts[0].shape[0], N * parts[0].shape[1])
    return call(
        weight_tile_kernel,
        out,
        (0, 0),
        [row_blocks(parts[0], steps)] * N,
        parts,
        after,
        grid=(steps,),
        out_specs=row_blocks(out, steps),
    )


def grad_tile_kernel(own, after, far, before, note0, note1, note2, note3, out, peaks):
    columns_kernel(here()[2], own, after, far, before, out)
    peaks[...] = peaks_in((note0, note1, note2, note3))


def grad_tile(parts):
    steps = 4
    rows, features = parts[0].shape[0] - NOTE, parts[0].shape[1]
    out = shape(rows, N * features)
    block = pl.BlockSpec((rows // steps, features), lambda i: (i, 0))
    return call(
        grad_tile_kernel,
        (out, shape(8, 128, dtype=F32)),
        (0, 0),
        [block] * N + [note_block(part) for part in parts],
        (*parts, *parts),
        grid=(steps,),
        out_specs=[row_blocks(out, steps), fixed(8, 128)],
    )


def later_kernel(value, out):
    out[...] = value[...]


def later(value, after):
    return call(
        later_kernel,
        shape(*value.shape, dtype=value.dtype),
        (0, 0),
        [IN_VMEM],
        (value,),
        after,
        out_specs=IN_VMEM,
    )


def histories_kernel(peaks, others, old_weight, old_act, new_weight, new_act):
    for row, old, new in ((1, old_weight, new_weight), (0, old_act, new_act)):
        new[:, 1:] = old[:, :-1]
        new[:, :1] = jnp.maximum(peaks[row : row + 1, :1], others[row : row + 1, :1])


def histories(peaks, others, old_weight, old_act):
    new = shape(*old_weight.shape, dtype=F32)
    return call(
        histories_kernel,
        (new, new),
        (0, 0),
        [IN_VMEM] * 4,
        (peaks, others, old_weight, old_act),
        out_specs=[IN_VMEM] * 2,
    )


def return_kernel(table, part0, part1, part2, part3, out0, out1, out2, out3):
    me, _, _ = here()
    tokens = out0.shape[0]
    for number, out in enumerate((out0, out1, out2, out3)):
        rows = pl.ds(pl.multiple_of(table[4 + number, me] * tokens, tokens), tokens)
        total = part0[rows, :].astype(F32) + part1[rows, :].astype(F32)
        total = total + (part2[rows, :].astype(F32) + part3[rows, :].astype(F32))
        out[...] = total.astype(BF16)


def return_blocks(parts, after):
    rows, features = parts[0].shape
    return call(
        return_kernel,
        (shape(rows // N, features),) * 4,
        (0, 0),
        [SCALARS] + [IN_VMEM] * 4,
        (jnp.asarray(TABLE), *parts),
        after,
        out_specs=[IN_VMEM] * 4,
    )


def add_kernel(part0, part1, part2, part3, out, token):
    total = part0[...].astype(F32) + part1[...].astype(F32)
    out[...] = (total + (part2[...].astype(F32) + part3[...].astype(F32))).astype(BF16)
    token[...] = jnp.zeros(token.shape, F32)


def add(parts):
    steps = 4
    rows = row_blocks(parts[0], steps)
    return call(
        add_kernel,
        (shape(*parts[0].shape), shape(8, 128, dtype=F32)),
        (0, 0),
        [rows] * 4,
        parts,
        grid=(steps,),
        out_specs=[rows, fixed(8, 128)],
    )


def merge_kernel(table, in0, in1, in2, in3, out):
    me, _, _ = here()
    width = in0.shape[1]
    for half in range(2):
        total = jnp.zeros(in0.shape, F32)
        for number, block in enumerate((in0, in1, in2, in3)):
            keep = (table[number, me] == half).astype(F32)
            total = total + block[...].astype(F32) * keep
        out[:, half * width : (half + 1) * width] = total.astype(BF16)


def merge(blocks):
    steps = 2
    out = shape(blocks[0].shape[0], 2 * blocks[0].shape[1])
    return call(
        merge_kernel,
        out,
        (0, 0),
        [SCALARS] + [row_blocks(blocks[0], steps)] * 4,
        (jnp.asarray(TABLE), *blocks),
        grid=(steps,),
        out_specs=row_blocks(out, steps),
    )


def finish_kernel(slope, silu, grad_act, grad_gate, grad_up):
    value = grad_act[...].astype(F32)
    grad_gate[...] = (value * slope[...].astype(F32)).astype(BF16)
    grad_up[...] = (value * silu[...].astype(F32)).astype(BF16)


def finish(slope, silu, grad_act):
    steps = 4
    rows = row_blocks(slope, steps)
    return call(
        finish_kernel,
        (shape(*slope.shape),) * 2,
        (0, 0),
        [rows] * 3,
        (slope, silu, grad_act),
        grid=(steps,),
        out_specs=[rows] * 2,
    )


def raise_peaks(peaks, bits):
    for bit in bits:
        peaks = jnp.maximum(peaks, send(peaks, [(n, n ^ (1 << bit)) for n in range(128)]))
    return peaks


def dot(left, right, dims):
    product = lax.dot_general(left, right, (dims, ((), ())), preferred_element_type=F32)
    return product.astype(BF16)


def on_device(gate_pre, up_pre, down_weight, grad_out, weight_history, act_history):
    features = down_weight.shape[1]
    _, feature_place, z = here()
    groups = token_groups()
    swap = [(n, n ^ 1) for n in range(128)]
    act_q, weight_q, peaks = activate(
        gate_pre, up_pre, down_weight, act_history[None], weight_history[None]
    )
    blocks = share(grad_out, peaks, send(peaks, swap))
    blocks = [
        send(block, [(edge[0], edge[1]) for edge in ROUNDS[number]])
        for number, block in enumerate(blocks)
    ]
    grad = place(blocks)
    act_q, weight_q = gate((act_q, weight_q), (grad,))
    act = lax.all_gather(act_q, AXES, axis=0, tiled=True, axis_index_groups=groups)
    weight_parts = ring_gather(weight_q, feature_ring)
    slope, silu, token = slopes(gate_pre, up_pre, (grad,))
    tile, peaks = grad_tile(ring_gather(grad, hidden_ring))
    weight = weight_tile(weight_parts, (token,))

    def block_of(array, number):
        return lax.dynamic_slice_in_dim(array, number % N * features, features, axis=1)

    grad_act = dot(tile, weight, ((1,), (1,)))
    grad_act = lax.psum_scatter(
        grad_act, AXES, scatter_dimension=0, tiled=True, axis_index_groups=groups
    )
    mixed = [dot(act, block_of(weight, z + step), ((1,), (0,))) for step in range(N)]
    act = gate((act,), mixed)[0]
    mixed = ring_exchange(mixed, hidden_ring)
    weight_grad = [
        dot(act, block_of(tile, feature_place + step), ((0,), (0,))) for step in range(N)
    ]
    weight_grad, token = add(ring_exchange(weight_grad, feature_ring))
    blocks = return_blocks(mixed, (token,))
    blocks = [
        send(block, [(edge[1], edge[0]) for edge in ROUNDS[number]])
        for number, block in enumerate(blocks)
    ]
    grad_gate, grad_up = finish(slope, silu, grad_act)
    peaks = raise_peaks(later(peaks, (token,)), (5, 6))
    new_weight, new_act = histories(
        peaks, send(peaks, swap), weight_history[None], act_history[None]
    )
    return (merge(blocks), grad_gate, grad_up, weight_grad, new_weight[0], new_act[0])


def solution(mesh):
    cube = Mesh(mesh.devices.reshape(N, N, N, 2), AXES)
    whole = P(("x", "y"), ("z", "c"))
    flipped = P(("z", "c"), ("x", "y"))
    return jax.shard_map(
        on_device,
        mesh=cube,
        in_specs=(whole, whole, flipped, whole, P(), P()),
        out_specs=(whole, whole, whole, flipped, P(), P()),
        check_vma=False,
    )
```

```python
import functools

import jax
import jax.numpy as jnp
import numpy as np
from jax import lax
from jax.experimental import pallas as pl
from jax.experimental.pallas import tpu as pltpu
from jax.sharding import Mesh, PartitionSpec as P

AXES = ("x", "y", "z", "c")
N = 4
BF16 = jnp.bfloat16
F32 = jnp.float32
VMEM_BYTES = 24 * 1024 * 1024
ANYWHERE = pl.BlockSpec(memory_space=pl.ANY)
SCALARS = pl.BlockSpec(memory_space=pltpu.SMEM)
IN_VMEM = pl.BlockSpec(memory_space=pltpu.VMEM)
IN_HBM = pl.BlockSpec(memory_space=pltpu.HBM)
NOTE = 16


def flat(x, y, z, c):
    return ((x % N * N + y % N) * N + z % N) * 2 + c


def places():
    return [(x, y, z, c) for x in range(N) for y in range(N) for z in range(N) for c in range(2)]


def token_ring(step):
    return [
        (flat(x, y, z, c), flat(x, y + step, z, c) if c == 0 else flat(x + step, y, z, c))
        for x, y, z, c in places()
    ]


def feature_ring(step):
    return [
        (flat(x, y, z, c), flat(x + step, y, z, c) if c == 0 else flat(x, y + step, z, c))
        for x, y, z, c in places()
    ]


def hidden_ring(step):
    return [(flat(x, y, z, c), flat(x, y, z + step, c)) for x, y, z, c in places()]


def token_groups():
    first = [[flat(x, y, z, 0) for y in range(N)] for x in range(N) for z in range(N)]
    second = [[flat(x, y, z, 1) for x in range(N)] for y in range(N) for z in range(N)]
    return first + second


def tile_edges():
    edges = []
    for x, y, z, c in places():
        for half in range(2):
            block = 2 * c + half
            edges.append((flat(x, y, z, c), flat(x, block, z, 0), half, y))
            edges.append((flat(x, y, z, c), flat(z, y, block, 1), half, x))
    return edges


def rounds():
    rest = tile_edges()
    out = []
    for _ in range(4):
        outgoing = {}
        for edge in rest:
            outgoing.setdefault(edge[0], []).append(edge)
        chosen = {}

        def augment(owner, seen):
            for edge in outgoing[owner]:
                if edge[1] in seen:
                    continue
                seen.add(edge[1])
                if edge[1] not in chosen or augment(chosen[edge[1]][0], seen):
                    chosen[edge[1]] = edge
                    return True
            return False

        for owner in range(128):
            augment(owner, set())
        picked = sorted(chosen.values())
        out.append(picked)
        rest = [edge for edge in rest if edge not in picked]
    return out


ROUNDS = rounds()
TABLE = np.zeros((8, 128), np.int32)
for number, picked in enumerate(ROUNDS):
    for owner, user, half, slot in picked:
        TABLE[number, owner] = half
        TABLE[4 + number, user] = slot


def send(value, pairs):
    return lax.ppermute(value, AXES, pairs)


def here():
    x, y, z, c = (lax.axis_index(name) for name in AXES)
    return flat(x, y, z, c), jnp.where(c == 0, x, y), z


def call(kernel, out_shape, cost, in_specs, operands, after=(), stored=(), vmem=VMEM_BYTES, **options):
    flops, moved = cost
    count = len(operands)
    extra = len(after) + len(stored)

    def body(*refs):
        kernel(*refs[:count], *refs[count + extra :])

    return pl.pallas_call(
        body,
        out_shape=out_shape,
        in_specs=list(in_specs) + [ANYWHERE] * len(after) + [IN_HBM] * len(stored),
        compiler_params=pltpu.CompilerParams(vmem_limit_bytes=vmem),
        cost_estimate=pl.CostEstimate(flops=flops, bytes_accessed=moved, transcendentals=0),
        **options,
    )(*operands, *after, *stored)


def shape(*dims, dtype=BF16):
    return jax.ShapeDtypeStruct(dims, dtype)


def ring_gather(own, ring):
    far = send(own, ring(2))
    return own, send(own, ring(-1)), far, send(own, ring(1))


def ring_exchange(parts, ring):
    far = send(parts[2], ring(2))
    return parts[0], send(parts[1], ring(1)), far, send(parts[3], ring(-1))


def peak_of(values):
    return jnp.max(jnp.abs(values), axis=0, keepdims=True)


def keep_peak(step, top, peak):
    @pl.when(step == 0)
    def _():
        top[...] = peak

    @pl.when(step > 0)
    def _():
        top[...] = jnp.maximum(top[...], peak)


def row_blocks(array, steps):
    return pl.BlockSpec((array.shape[0] // steps, array.shape[1]), lambda i: (i, 0))


def fixed(*dims):
    return pl.BlockSpec(dims, lambda i: (0, 0))


def note_of(peaks, width):
    row = lax.broadcasted_iota(jnp.int32, (NOTE, width), 0)
    note = jnp.zeros((NOTE, width), F32)
    for number in range(2):
        rest = jnp.broadcast_to(peaks[number : number + 1, :1], (NOTE, width))
        for piece in range(3):
            value = rest.astype(BF16).astype(F32)
            note = jnp.where(row == 3 * number + piece, value, note)
            rest = rest - value
    return note.astype(BF16)


def peaks_in(notes):
    best = []
    for number in range(2):
        values = []
        for note in notes:
            note = note[...].astype(F32)
            pieces = [note[3 * number + piece : 3 * number + piece + 1, :128] for piece in range(3)]
            values.append(pieces[0] + pieces[1] + pieces[2])
        best.append(functools.reduce(jnp.maximum, values))
    row = lax.broadcasted_iota(jnp.int32, (8, 128), 0)
    return jnp.where(row == 0, jnp.broadcast_to(best[0], (8, 128)), jnp.broadcast_to(best[1], (8, 128)))


def note_block(array):
    last = array.shape[0] // NOTE - 1
    return pl.BlockSpec((NOTE, array.shape[1]), lambda *i: (last, 0))


def share_kernel(table, grad, peaks, others, out0, out1, out2, out3):
    me, _, _ = here()
    tokens, width = grad.shape[0], grad.shape[1] // 2
    note = note_of(jnp.maximum(peaks[...], others[...]), width)
    for number, out in enumerate((out0, out1, out2, out3)):
        half = table[number, me]

        @pl.when(half == 0)
        def _():
            out[:tokens, :] = grad[:, :width]

        @pl.when(half == 1)
        def _():
            out[:tokens, :] = grad[:, width:]

        out[tokens:, :] = note


def share(grad, peaks, others):
    block = shape(grad.shape[0] + NOTE, grad.shape[1] // 2)
    return call(
        share_kernel,
        (block, block, block, block),
        (0, 0),
        [SCALARS] + [IN_VMEM] * 3,
        (jnp.asarray(TABLE), grad, peaks, others),
        out_specs=[IN_VMEM] * 4,
    )


def clip_kernel(weight, history, weight_q, peak, top):
    step = pl.program_id(0)
    weight_v = weight[...].astype(F32)
    limit = jnp.max(history[...], axis=1, keepdims=True)
    weight_q[...] = jnp.clip(weight_v, -limit, limit).astype(BF16)
    keep_peak(step, top, peak_of(weight_v))

    @pl.when(step == pl.num_programs(0) - 1)
    def _():
        peak[...] = jnp.broadcast_to(jnp.max(top[...], axis=1, keepdims=True), peak.shape)


def clip_weight(weight, history):
    steps = 2
    rows = row_blocks(weight, steps)
    return call(
        clip_kernel,
        (shape(*weight.shape), shape(8, 128, dtype=F32)),
        (0, 0),
        [rows, fixed(1, history.shape[1])],
        (weight, history),
        grid=(steps,),
        out_specs=[rows, fixed(8, 128)],
        scratch_shapes=[pltpu.VMEM((1, weight.shape[1]), F32)],
    )


def activate_kernel(gate, up, weight_peak, history, act_q, peaks, top):
    step = pl.program_id(0)
    gate_v = gate[...].astype(F32)
    act = gate_v * jax.nn.sigmoid(gate_v) * up[...].astype(F32)
    limit = jnp.max(history[...], axis=1, keepdims=True)
    act_q[...] = jnp.clip(act, -limit, limit).astype(BF16)
    keep_peak(step, top, peak_of(act))

    @pl.when(step == pl.num_programs(0) - 1)
    def _():
        row = lax.broadcasted_iota(jnp.int32, peaks.shape, 0)
        act_peak = jnp.broadcast_to(jnp.max(top[...], axis=1, keepdims=True), peaks.shape)
        peaks[...] = jnp.where(row == 0, act_peak, weight_peak[...])


def activate(gate, up, weight_peak, history):
    steps = 8
    rows = row_blocks(gate, steps)
    return call(
        activate_kernel,
        (shape(*gate.shape), shape(8, 128, dtype=F32)),
        (0, 0),
        [rows, rows, fixed(8, 128), fixed(1, history.shape[1])],
        (gate, up, weight_peak, history),
        grid=(steps,),
        out_specs=[rows, fixed(8, 128)],
        scratch_shapes=[pltpu.VMEM((1, gate.shape[1]), F32)],
    )


def slopes_kernel(gate, up, slope, silu, token):
    gate_v = gate[...].astype(F32)
    sigm = jax.nn.sigmoid(gate_v)
    slope[...] = (up[...].astype(F32) * sigm * (1.0 + gate_v * (1.0 - sigm))).astype(BF16)
    silu[...] = (gate_v * sigm).astype(BF16)
    token[...] = jnp.zeros(token.shape, F32)


def slopes(gate, up, after):
    steps = 8
    rows = row_blocks(gate, steps)
    return call(
        slopes_kernel,
        (shape(*gate.shape), shape(*gate.shape), shape(8, 128, dtype=F32)),
        (0, 0),
        [rows, rows],
        (gate, up),
        after,
        grid=(steps,),
        out_specs=[rows, rows, fixed(8, 128)],
    )


def place_kernel(table, in0, in1, in2, in3, out):
    me, _, _ = here()
    rows = in0.shape[0] - NOTE
    for number, block in enumerate((in0, in1, in2, in3)):
        start = pl.multiple_of(table[4 + number, me] * rows, rows)
        out[pl.ds(start, rows), :] = block[:rows, :]
    peaks = peaks_in([block[rows:, :] for block in (in0, in1, in2, in3)])
    out[4 * rows :, :] = note_of(peaks, out.shape[1])


def place(blocks):
    rows, features = blocks[0].shape
    return call(
        place_kernel,
        shape(4 * (rows - NOTE) + NOTE, features),
        (0, 0),
        [SCALARS] + [IN_VMEM] * 4,
        (jnp.asarray(TABLE), *blocks),
        out_specs=IN_VMEM,
    )


def gate_kernel(*refs):
    pass


def gate(values, after=(), stored=()):
    count = len(values)
    return call(
        gate_kernel,
        tuple(shape(*value.shape) for value in values),
        (0, 0),
        [ANYWHERE] * count,
        values,
        after,
        stored,
        vmem=1024 * 1024,
        out_specs=[ANYWHERE] * count,
        input_output_aliases={number: number for number in range(count)},
    )


def columns_kernel(place, own, after, far, before, out):
    width = own.shape[1]
    for step, block in enumerate((own, after, far, before)):
        column = (place + step) % N * width
        if not isinstance(column, int):
            column = pl.multiple_of(column, width)
        out[:, pl.ds(column, width)] = block[...]


def half_blocks(steps, dims):
    first = pl.BlockSpec(dims, lambda i: (jnp.minimum(i, steps // 2 - 1), 0))
    second = pl.BlockSpec(dims, lambda i: (jnp.maximum(i - steps // 2, 0), 0))
    return [first, second]


def weight_tile_kernel(own, after, top, bottom, before, out):
    place = here()[1]
    step = pl.program_id(0)

    @pl.when(step < pl.num_programs(0) // 2)
    def _():
        columns_kernel(place, own, after, top, before, out)

    @pl.when(step >= pl.num_programs(0) // 2)
    def _():
        columns_kernel(place, own, after, bottom, before, out)


def weight_tile(*parts):
    steps = 4
    hidden, features = parts[0].shape
    dims = (hidden // steps, features)
    block = pl.BlockSpec(dims, lambda i: (i, 0))
    out = shape(hidden, N * features)
    return call(
        weight_tile_kernel,
        out,
        (0, 0),
        [block, block, *half_blocks(steps, dims), block],
        parts,
        grid=(steps,),
        out_specs=row_blocks(out, steps),
    )


def raise_kernel(after, before, top, bottom, out_after, out_before):
    rows = top.shape[0]
    out_after[:rows, :] = (after[:rows, :].astype(F32) + top[...].astype(F32)).astype(BF16)
    out_after[rows:, :] = after[rows:, :]
    out_before[:rows, :] = before[:rows, :]
    out_before[rows:, :] = (before[rows:, :].astype(F32) + bottom[...].astype(F32)).astype(BF16)


def add_halves(after, before, top, bottom):
    whole = shape(*after.shape)
    return call(
        raise_kernel,
        (whole, whole),
        (0, 0),
        [IN_VMEM] * 4,
        (after, before, top, bottom),
        out_specs=[IN_VMEM] * 2,
    )


def grad_tile_kernel(own, after, top, bottom, before, note0, note1, note2, note3, out, peaks):
    place = here()[2]
    step = pl.program_id(0)

    @pl.when(step < pl.num_programs(0) // 2)
    def _():
        columns_kernel(place, own, after, top, before, out)

    @pl.when(step >= pl.num_programs(0) // 2)
    def _():
        columns_kernel(place, own, after, bottom, before, out)

    peaks[...] = peaks_in((note0, note1, note2, note3))


def grad_tile(own, after, top, bottom, before, order):
    steps = 4
    rows, features = own.shape[0] - NOTE, own.shape[1]
    out = shape(rows, N * features)
    dims = (rows // steps, features)
    block = pl.BlockSpec(dims, lambda i: (i, 0))
    noted = (own, after, bottom, before)
    return call(
        grad_tile_kernel,
        (out, shape(8, 128, dtype=F32)),
        (0, 0),
        [block, block, *half_blocks(steps, dims), block] + [note_block(part) for part in noted],
        (own, after, top, bottom, before, *noted),
        order,
        grid=(steps,),
        out_specs=[row_blocks(out, steps), fixed(8, 128)],
    )


def later_kernel(value, out):
    out[...] = value[...]


def later(value, after):
    return call(
        later_kernel,
        shape(*value.shape, dtype=value.dtype),
        (0, 0),
        [IN_VMEM],
        (value,),
        after,
        out_specs=IN_VMEM,
    )


def histories_kernel(peaks, others, old_weight, old_act, new_weight, new_act):
    for row, old, new in ((1, old_weight, new_weight), (0, old_act, new_act)):
        new[:, 1:] = old[:, :-1]
        new[:, :1] = jnp.maximum(peaks[row : row + 1, :1], others[row : row + 1, :1])


def histories(peaks, others, old_weight, old_act):
    new = shape(*old_weight.shape, dtype=F32)
    return call(
        histories_kernel,
        (new, new),
        (0, 0),
        [IN_VMEM] * 4,
        (peaks, others, old_weight, old_act),
        out_specs=[IN_VMEM] * 2,
    )


def return_kernel(table, own, before, after, out0, out1, out2, out3):
    me, _, _ = here()
    tokens = out0.shape[0]
    for number, out in enumerate((out0, out1, out2, out3)):
        rows = pl.ds(pl.multiple_of(table[4 + number, me] * tokens, tokens), tokens)
        total = own[rows, :].astype(F32) + before[rows, :].astype(F32) + after[rows, :].astype(F32)
        out[...] = total.astype(BF16)


def return_blocks(parts, after):
    rows, features = parts[0].shape
    return call(
        return_kernel,
        (shape(rows // N, features),) * 4,
        (0, 0),
        [SCALARS] + [IN_VMEM] * 3,
        (jnp.asarray(TABLE), *parts),
        after,
        out_specs=[IN_VMEM] * 4,
    )


def add_kernel(part0, part1, part2, part3, out, token):
    total = part0[...].astype(F32) + part1[...].astype(F32)
    out[...] = (total + (part2[...].astype(F32) + part3[...].astype(F32))).astype(BF16)
    token[...] = jnp.zeros(token.shape, F32)


def add(parts):
    steps = 4
    rows = row_blocks(parts[0], steps)
    return call(
        add_kernel,
        (shape(*parts[0].shape), shape(8, 128, dtype=F32)),
        (0, 0),
        [rows] * 4,
        parts,
        grid=(steps,),
        out_specs=[rows, fixed(8, 128)],
    )


def merge_kernel(table, in0, in1, in2, in3, out):
    me, _, _ = here()
    width = in0.shape[1]
    for half in range(2):
        total = jnp.zeros(in0.shape, F32)
        for number, block in enumerate((in0, in1, in2, in3)):
            keep = (table[number, me] == half).astype(F32)
            total = total + block[...].astype(F32) * keep
        out[:, half * width : (half + 1) * width] = total.astype(BF16)


def merge(blocks):
    steps = 2
    out = shape(blocks[0].shape[0], 2 * blocks[0].shape[1])
    return call(
        merge_kernel,
        out,
        (0, 0),
        [SCALARS] + [row_blocks(blocks[0], steps)] * 4,
        (jnp.asarray(TABLE), *blocks),
        grid=(steps,),
        out_specs=row_blocks(out, steps),
    )


def finish_kernel(slope, silu, grad_act, grad_gate, grad_up):
    value = grad_act[...].astype(F32)
    grad_gate[...] = (value * slope[...].astype(F32)).astype(BF16)
    grad_up[...] = (value * silu[...].astype(F32)).astype(BF16)


def finish(slope, silu, grad_act):
    steps = 4
    rows = row_blocks(slope, steps)
    return call(
        finish_kernel,
        (shape(*slope.shape),) * 2,
        (0, 0),
        [rows] * 3,
        (slope, silu, grad_act),
        grid=(steps,),
        out_specs=[rows] * 2,
    )


def raise_peaks(peaks, bits):
    for bit in bits:
        peaks = jnp.maximum(peaks, send(peaks, [(n, n ^ (1 << bit)) for n in range(128)]))
    return peaks


def dot(left, right, dims):
    product = lax.dot_general(left, right, (dims, ((), ())), preferred_element_type=F32)
    return product.astype(BF16)


def on_device(gate_pre, up_pre, down_weight, grad_out, weight_history, act_history):
    _, feature_place, z = here()
    groups = token_groups()
    swap = [(n, n ^ 1) for n in range(128)]
    weight_q, weight_peak = clip_weight(down_weight, weight_history[None])
    weight_before, weight_after = send(weight_q, feature_ring(1)), send(weight_q, feature_ring(-1))
    half = weight_q.shape[0] // 2
    weight = weight_tile(
        weight_q,
        weight_after,
        send(weight_before[:half], feature_ring(1)),
        send(weight_after[half:], feature_ring(-1)),
        weight_before,
    )
    act_q, peaks = activate(gate_pre, up_pre, weight_peak, act_history[None])
    blocks = share(grad_out, peaks, send(peaks, swap))
    blocks = [
        send(block, [(edge[0], edge[1]) for edge in ROUNDS[number]])
        for number, block in enumerate(blocks)
    ]
    grad = place(blocks)
    (act_q,) = gate((act_q,), (grad,))
    act = lax.all_gather(act_q, AXES, axis=0, tiled=True, axis_index_groups=groups)
    slope, silu, token = slopes(gate_pre, up_pre, (grad,))
    before, after = send(grad, hidden_ring(1)), send(grad, hidden_ring(-1))
    half = (grad.shape[0] - NOTE) // 2
    top, bottom = send(before[:half], hidden_ring(1)), send(after[half:], hidden_ring(-1))

    def block_of(array, number):
        size = array.shape[1] // N
        return lax.dynamic_slice_in_dim(array, number % N * size, size, axis=1)

    tile, peaks = grad_tile(grad, after, top, bottom, before, (token,))
    grad_act = dot(tile, weight, ((1,), (1,)))
    grad_act = lax.psum_scatter(
        grad_act, AXES, scatter_dimension=0, tiled=True, axis_index_groups=groups
    )
    half = act.shape[0] // 2
    mixed = [dot(act, block_of(weight, z + step), ((1,), (0,))) for step in (0, 1, 3)]
    far = block_of(weight, z + 2)
    mixed_top = send(dot(act[:half], far, ((1,), (0,))), hidden_ring(1))
    mixed_bottom = send(dot(act[half:], far, ((1,), (0,))), hidden_ring(-1))
    mixed_after, mixed_before = add_halves(mixed[1], mixed[2], mixed_top, mixed_bottom)
    (act,) = gate((act,), (mixed[0], mixed_after))
    weight_grad = [
        dot(act, block_of(tile, feature_place + step), ((0,), (0,))) for step in range(N)
    ]
    weight_grad, _ = add(ring_exchange(weight_grad, feature_ring))
    mixed = (mixed[0], send(mixed_after, hidden_ring(1)), send(mixed_before, hidden_ring(-1)))
    blocks = return_blocks(mixed, ())
    blocks = [
        send(block, [(edge[1], edge[0]) for edge in ROUNDS[number]])
        for number, block in enumerate(blocks)
    ]
    peaks = raise_peaks(later(peaks, blocks[:1]), (5, 6))
    grad_gate, grad_up = finish(slope, silu, grad_act)
    new_weight, new_act = histories(
        peaks, send(peaks, swap), weight_history[None], act_history[None]
    )
    return (merge(blocks), grad_gate, grad_up, weight_grad, new_weight[0], new_act[0])


def solution(mesh):
    cube = Mesh(mesh.devices.reshape(N, N, N, 2), AXES)
    whole = P(("x", "y"), ("z", "c"))
    flipped = P(("z", "c"), ("x", "y"))
    return jax.shard_map(
        on_device,
        mesh=cube,
        in_specs=(whole, whole, flipped, whole, P(), P()),
        out_specs=(whole, whole, whole, flipped, P(), P()),
        check_vma=False,
    )
```

```python
import functools

import jax
import jax.numpy as jnp
import numpy as np
from jax import lax
from jax.experimental import pallas as pl
from jax.experimental.pallas import tpu as pltpu
from jax.sharding import Mesh, PartitionSpec as P

AXES = ("x", "y", "z", "c")
N = 4
BF16 = jnp.bfloat16
F32 = jnp.float32
VMEM_BYTES = 24 * 1024 * 1024
ANYWHERE = pl.BlockSpec(memory_space=pl.ANY)
SCALARS = pl.BlockSpec(memory_space=pltpu.SMEM)
IN_VMEM = pl.BlockSpec(memory_space=pltpu.VMEM)
IN_HBM = pl.BlockSpec(memory_space=pltpu.HBM)
NOTE = 16


def flat(x, y, z, c):
    return ((x % N * N + y % N) * N + z % N) * 2 + c


def places():
    return [(x, y, z, c) for x in range(N) for y in range(N) for z in range(N) for c in range(2)]


def token_ring(step):
    return [
        (flat(x, y, z, c), flat(x, y + step, z, c) if c == 0 else flat(x + step, y, z, c))
        for x, y, z, c in places()
    ]


def feature_ring(step):
    return [
        (flat(x, y, z, c), flat(x + step, y, z, c) if c == 0 else flat(x, y + step, z, c))
        for x, y, z, c in places()
    ]


def hidden_ring(step):
    return [(flat(x, y, z, c), flat(x, y, z + step, c)) for x, y, z, c in places()]


def token_groups():
    first = [[flat(x, y, z, 0) for y in range(N)] for x in range(N) for z in range(N)]
    second = [[flat(x, y, z, 1) for x in range(N)] for y in range(N) for z in range(N)]
    return first + second


def tile_edges():
    edges = []
    for x, y, z, c in places():
        for half in range(2):
            block = 2 * c + half
            edges.append((flat(x, y, z, c), flat(x, block, z, 0), half, y))
            edges.append((flat(x, y, z, c), flat(z, y, block, 1), half, x))
    return edges


def rounds():
    rest = tile_edges()
    out = []
    for _ in range(4):
        outgoing = {}
        for edge in rest:
            outgoing.setdefault(edge[0], []).append(edge)
        chosen = {}

        def augment(owner, seen):
            for edge in outgoing[owner]:
                if edge[1] in seen:
                    continue
                seen.add(edge[1])
                if edge[1] not in chosen or augment(chosen[edge[1]][0], seen):
                    chosen[edge[1]] = edge
                    return True
            return False

        for owner in range(128):
            augment(owner, set())
        picked = sorted(chosen.values())
        out.append(picked)
        rest = [edge for edge in rest if edge not in picked]
    return out


ROUNDS = rounds()
TABLE = np.zeros((8, 128), np.int32)
for number, picked in enumerate(ROUNDS):
    for owner, user, half, slot in picked:
        TABLE[number, owner] = half
        TABLE[4 + number, user] = slot


def send(value, pairs):
    return lax.ppermute(value, AXES, pairs)


def here():
    x, y, z, c = (lax.axis_index(name) for name in AXES)
    return flat(x, y, z, c), jnp.where(c == 0, x, y), z


def call(kernel, out_shape, cost, in_specs, operands, after=(), stored=(), vmem=VMEM_BYTES, **options):
    flops, moved = cost
    count = len(operands)
    extra = len(after) + len(stored)

    def body(*refs):
        kernel(*refs[:count], *refs[count + extra :])

    return pl.pallas_call(
        body,
        out_shape=out_shape,
        in_specs=list(in_specs) + [ANYWHERE] * len(after) + [IN_HBM] * len(stored),
        compiler_params=pltpu.CompilerParams(vmem_limit_bytes=vmem),
        cost_estimate=pl.CostEstimate(flops=flops, bytes_accessed=moved, transcendentals=0),
        **options,
    )(*operands, *after, *stored)


def shape(*dims, dtype=BF16):
    return jax.ShapeDtypeStruct(dims, dtype)


def ring_gather(own, ring):
    far = send(own, ring(2))
    return own, send(own, ring(-1)), far, send(own, ring(1))


def ring_exchange(parts, ring):
    far = send(parts[2], ring(2))
    return parts[0], send(parts[1], ring(1)), far, send(parts[3], ring(-1))


def peak_of(values):
    return jnp.max(jnp.abs(values), axis=0, keepdims=True)


def keep_peak(step, top, peak):
    @pl.when(step == 0)
    def _():
        top[...] = peak

    @pl.when(step > 0)
    def _():
        top[...] = jnp.maximum(top[...], peak)


def row_blocks(array, steps):
    return pl.BlockSpec((array.shape[0] // steps, array.shape[1]), lambda i: (i, 0))


def fixed(*dims):
    return pl.BlockSpec(dims, lambda i: (0, 0))


def note_of(peaks, width):
    row = lax.broadcasted_iota(jnp.int32, (NOTE, width), 0)
    note = jnp.zeros((NOTE, width), F32)
    for number in range(2):
        rest = jnp.broadcast_to(peaks[number : number + 1, :1], (NOTE, width))
        for piece in range(3):
            value = rest.astype(BF16).astype(F32)
            note = jnp.where(row == 3 * number + piece, value, note)
            rest = rest - value
    return note.astype(BF16)


def peaks_in(notes):
    best = []
    for number in range(2):
        values = []
        for note in notes:
            note = note[...].astype(F32)
            pieces = [note[3 * number + piece : 3 * number + piece + 1, :128] for piece in range(3)]
            values.append(pieces[0] + pieces[1] + pieces[2])
        best.append(functools.reduce(jnp.maximum, values))
    row = lax.broadcasted_iota(jnp.int32, (8, 128), 0)
    return jnp.where(row == 0, jnp.broadcast_to(best[0], (8, 128)), jnp.broadcast_to(best[1], (8, 128)))


def note_block(array):
    last = array.shape[0] // NOTE - 1
    return pl.BlockSpec((NOTE, array.shape[1]), lambda *i: (last, 0))


def share_kernel(table, grad, peaks, others, out0, out1, out2, out3):
    me, _, _ = here()
    tokens, width = grad.shape[0], grad.shape[1] // 2
    note = note_of(jnp.maximum(peaks[...], others[...]), width)
    for number, out in enumerate((out0, out1, out2, out3)):
        half = table[number, me]

        @pl.when(half == 0)
        def _():
            out[:tokens, :] = grad[:, :width]

        @pl.when(half == 1)
        def _():
            out[:tokens, :] = grad[:, width:]

        out[tokens:, :] = note


def share(grad, peaks, others):
    block = shape(grad.shape[0] + NOTE, grad.shape[1] // 2)
    return call(
        share_kernel,
        (block, block, block, block),
        (0, 0),
        [SCALARS] + [IN_VMEM] * 3,
        (jnp.asarray(TABLE), grad, peaks, others),
        out_specs=[IN_VMEM] * 4,
    )


def clip_kernel(weight, history, weight_q, peak, top):
    step = pl.program_id(0)
    weight_v = weight[...].astype(F32)
    limit = jnp.max(history[...], axis=1, keepdims=True)
    weight_q[...] = jnp.clip(weight_v, -limit, limit).astype(BF16)
    keep_peak(step, top, peak_of(weight_v))

    @pl.when(step == pl.num_programs(0) - 1)
    def _():
        peak[...] = jnp.broadcast_to(jnp.max(top[...], axis=1, keepdims=True), peak.shape)


def clip_weight(weight, history):
    steps = 2
    rows = row_blocks(weight, steps)
    return call(
        clip_kernel,
        (shape(*weight.shape), shape(8, 128, dtype=F32)),
        (0, 0),
        [rows, fixed(1, history.shape[1])],
        (weight, history),
        grid=(steps,),
        out_specs=[rows, fixed(8, 128)],
        scratch_shapes=[pltpu.VMEM((1, weight.shape[1]), F32)],
    )


def activate_kernel(gate, up, weight_peak, history, act_q, peaks, top):
    step = pl.program_id(0)
    gate_v = gate[...].astype(F32)
    act = gate_v * jax.nn.sigmoid(gate_v) * up[...].astype(F32)
    limit = jnp.max(history[...], axis=1, keepdims=True)
    act_q[...] = jnp.clip(act, -limit, limit).astype(BF16)
    keep_peak(step, top, peak_of(act))

    @pl.when(step == pl.num_programs(0) - 1)
    def _():
        row = lax.broadcasted_iota(jnp.int32, peaks.shape, 0)
        act_peak = jnp.broadcast_to(jnp.max(top[...], axis=1, keepdims=True), peaks.shape)
        peaks[...] = jnp.where(row == 0, act_peak, weight_peak[...])


def activate(gate, up, weight_peak, history):
    steps = 8
    rows = row_blocks(gate, steps)
    return call(
        activate_kernel,
        (shape(*gate.shape), shape(8, 128, dtype=F32)),
        (0, 0),
        [rows, rows, fixed(8, 128), fixed(1, history.shape[1])],
        (gate, up, weight_peak, history),
        grid=(steps,),
        out_specs=[rows, fixed(8, 128)],
        scratch_shapes=[pltpu.VMEM((1, gate.shape[1]), F32)],
    )


def slopes_kernel(gate, up, slope, silu, token):
    gate_v = gate[...].astype(F32)
    sigm = jax.nn.sigmoid(gate_v)
    slope[...] = (up[...].astype(F32) * sigm * (1.0 + gate_v * (1.0 - sigm))).astype(BF16)
    silu[...] = (gate_v * sigm).astype(BF16)
    token[...] = jnp.zeros(token.shape, F32)


def slopes(gate, up, after):
    steps = 8
    rows = row_blocks(gate, steps)
    return call(
        slopes_kernel,
        (shape(*gate.shape), shape(*gate.shape), shape(8, 128, dtype=F32)),
        (0, 0),
        [rows, rows],
        (gate, up),
        after,
        grid=(steps,),
        out_specs=[rows, rows, fixed(8, 128)],
    )


def place_kernel(table, in0, in1, in2, in3, out, peaks):
    me, _, _ = here()
    rows = in0.shape[0] - NOTE
    for number, block in enumerate((in0, in1, in2, in3)):
        start = pl.multiple_of(table[4 + number, me] * rows, rows)
        out[pl.ds(start, rows), :] = block[:rows, :]
    peaks[...] = peaks_in([block[rows:, :] for block in (in0, in1, in2, in3)])


def place(blocks):
    rows, features = blocks[0].shape
    return call(
        place_kernel,
        (shape(4 * (rows - NOTE), features), shape(8, 128, dtype=F32)),
        (0, 0),
        [SCALARS] + [IN_VMEM] * 4,
        (jnp.asarray(TABLE), *blocks),
        out_specs=[IN_VMEM] * 2,
    )


def stamp_kernel(weight, peaks, out):
    rows = weight.shape[0]
    out[:rows, :] = weight[...]
    out[rows:, :] = note_of(peaks[...], weight.shape[1])


def stamp(weight, peaks):
    return call(
        stamp_kernel,
        shape(weight.shape[0] + NOTE, weight.shape[1]),
        (0, 0),
        [IN_VMEM] * 2,
        (weight, peaks),
        out_specs=IN_VMEM,
    )


def gate_kernel(*refs):
    pass


def gate(values, after=(), stored=()):
    count = len(values)
    return call(
        gate_kernel,
        tuple(shape(*value.shape) for value in values),
        (0, 0),
        [ANYWHERE] * count,
        values,
        after,
        stored,
        vmem=1024 * 1024,
        out_specs=[ANYWHERE] * count,
        input_output_aliases={number: number for number in range(count)},
    )


def columns_kernel(place, own, after, far, before, out):
    width = own.shape[1]
    for step, block in enumerate((own, after, far, before)):
        column = (place + step) % N * width
        if not isinstance(column, int):
            column = pl.multiple_of(column, width)
        out[:, pl.ds(column, width)] = block[...]


def half_blocks(steps, dims):
    first = pl.BlockSpec(dims, lambda i: (jnp.minimum(i, steps // 2 - 1), 0))
    second = pl.BlockSpec(dims, lambda i: (jnp.maximum(i - steps // 2, 0), 0))
    return [first, second]


def weight_tile_kernel(own, after, top, bottom, before, note0, note1, note2, note3, out, peaks):
    place = here()[1]
    step = pl.program_id(0)

    @pl.when(step < pl.num_programs(0) // 2)
    def _():
        columns_kernel(place, own, after, top, before, out)

    @pl.when(step >= pl.num_programs(0) // 2)
    def _():
        columns_kernel(place, own, after, bottom, before, out)

    peaks[...] = peaks_in((note0, note1, note2, note3))


def weight_tile(own, after, top, bottom, before):
    steps = 4
    hidden, features = own.shape[0] - NOTE, own.shape[1]
    dims = (hidden // steps, features)
    block = pl.BlockSpec(dims, lambda i: (i, 0))
    out = shape(hidden, N * features)
    noted = (own, after, bottom, before)
    return call(
        weight_tile_kernel,
        (out, shape(8, 128, dtype=F32)),
        (0, 0),
        [block, block, *half_blocks(steps, dims), block] + [note_block(part) for part in noted],
        (own, after, top, bottom, before, *noted),
        grid=(steps,),
        out_specs=[row_blocks(out, steps), fixed(8, 128)],
    )


def raise_kernel(after, before, top, bottom, out_after, out_before):
    rows = top.shape[0]
    out_after[:rows, :] = (after[:rows, :].astype(F32) + top[...].astype(F32)).astype(BF16)
    out_after[rows:, :] = after[rows:, :]
    out_before[:rows, :] = before[:rows, :]
    out_before[rows:, :] = (before[rows:, :].astype(F32) + bottom[...].astype(F32)).astype(BF16)


def add_halves(after, before, top, bottom, order):
    whole = shape(*after.shape)
    return call(
        raise_kernel,
        (whole, whole),
        (0, 0),
        [IN_VMEM] * 4,
        (after, before, top, bottom),
        order,
        out_specs=[IN_VMEM] * 2,
    )


def grad_tile_kernel(own, after, top, bottom, before, out):
    place = here()[2]
    step = pl.program_id(0)

    @pl.when(step < pl.num_programs(0) // 2)
    def _():
        columns_kernel(place, own, after, top, before, out)

    @pl.when(step >= pl.num_programs(0) // 2)
    def _():
        columns_kernel(place, own, after, bottom, before, out)


def grad_tile(own, after, top, bottom, before, order):
    steps = 4
    rows, features = own.shape
    dims = (rows // steps, features)
    block = pl.BlockSpec(dims, lambda i: (i, 0))
    out = shape(rows, N * features)
    return call(
        grad_tile_kernel,
        out,
        (0, 0),
        [block, block, *half_blocks(steps, dims), block],
        (own, after, top, bottom, before),
        order,
        grid=(steps,),
        out_specs=row_blocks(out, steps),
    )


def histories_kernel(peaks, others, old_weight, old_act, new_weight, new_act):
    for row, old, new in ((1, old_weight, new_weight), (0, old_act, new_act)):
        new[:, 1:] = old[:, :-1]
        new[:, :1] = jnp.maximum(peaks[row : row + 1, :1], others[row : row + 1, :1])


def histories(peaks, others, old_weight, old_act):
    new = shape(*old_weight.shape, dtype=F32)
    return call(
        histories_kernel,
        (new, new),
        (0, 0),
        [IN_VMEM] * 4,
        (peaks, others, old_weight, old_act),
        out_specs=[IN_VMEM] * 2,
    )


def return_kernel(table, own, before, after, peaks, out0, out1, out2, out3):
    me, _, _ = here()
    tokens = out0.shape[0] - NOTE
    note = note_of(peaks[...], out0.shape[1])
    for number, out in enumerate((out0, out1, out2, out3)):
        rows = pl.ds(pl.multiple_of(table[4 + number, me] * tokens, tokens), tokens)
        total = own[rows, :].astype(F32) + before[rows, :].astype(F32) + after[rows, :].astype(F32)
        out[:tokens, :] = total.astype(BF16)
        out[tokens:, :] = note


def return_blocks(parts, peaks):
    rows, features = parts[0].shape
    return call(
        return_kernel,
        (shape(rows // N + NOTE, features),) * 4,
        (0, 0),
        [SCALARS] + [IN_VMEM] * 4,
        (jnp.asarray(TABLE), *parts, peaks),
        out_specs=[IN_VMEM] * 4,
    )


def read_kernel(note0, note1, note2, note3, peaks):
    peaks[...] = peaks_in((note0, note1, note2, note3))


def read_notes(blocks):
    return call(
        read_kernel,
        shape(8, 128, dtype=F32),
        (0, 0),
        [note_block(block) for block in blocks],
        blocks,
        grid=(1,),
        out_specs=fixed(8, 128),
    )


def add_kernel(part0, part1, part2, part3, out, token):
    total = part0[...].astype(F32) + part1[...].astype(F32)
    out[...] = (total + (part2[...].astype(F32) + part3[...].astype(F32))).astype(BF16)
    token[...] = jnp.zeros(token.shape, F32)


def add(parts):
    steps = 4
    rows = row_blocks(parts[0], steps)
    return call(
        add_kernel,
        (shape(*parts[0].shape), shape(8, 128, dtype=F32)),
        (0, 0),
        [rows] * 4,
        parts,
        grid=(steps,),
        out_specs=[rows, fixed(8, 128)],
    )


def merge_kernel(table, in0, in1, in2, in3, out):
    me, _, _ = here()
    width = in0.shape[1]
    for half in range(2):
        total = jnp.zeros(in0.shape, F32)
        for number, block in enumerate((in0, in1, in2, in3)):
            keep = (table[number, me] == half).astype(F32)
            total = total + block[...].astype(F32) * keep
        out[:, half * width : (half + 1) * width] = total.astype(BF16)


def merge(blocks, after):
    steps = 2
    tokens, features = blocks[0].shape[0] - NOTE, blocks[0].shape[1]
    block = pl.BlockSpec((tokens // steps, features), lambda i: (i, 0))
    out = shape(tokens, 2 * features)
    return call(
        merge_kernel,
        out,
        (0, 0),
        [SCALARS] + [block] * 4,
        (jnp.asarray(TABLE), *blocks),
        after,
        grid=(steps,),
        out_specs=row_blocks(out, steps),
    )


def finish_kernel(slope, silu, grad_act, grad_gate, grad_up, token):
    value = grad_act[...].astype(F32)
    grad_gate[...] = (value * slope[...].astype(F32)).astype(BF16)
    grad_up[...] = (value * silu[...].astype(F32)).astype(BF16)
    token[...] = jnp.zeros(token.shape, F32)


def finish(slope, silu, grad_act):
    steps = 4
    rows = row_blocks(slope, steps)
    return call(
        finish_kernel,
        (shape(*slope.shape), shape(*slope.shape), shape(8, 128, dtype=F32)),
        (0, 0),
        [rows] * 3,
        (slope, silu, grad_act),
        grid=(steps,),
        out_specs=[rows, rows, fixed(8, 128)],
    )


def dot(left, right, dims):
    product = lax.dot_general(left, right, (dims, ((), ())), preferred_element_type=F32)
    return product.astype(BF16)


def on_device(gate_pre, up_pre, down_weight, grad_out, weight_history, act_history):
    _, feature_place, z = here()
    groups = token_groups()
    swap = [(n, n ^ 1) for n in range(128)]
    weight_q, weight_peak = clip_weight(down_weight, weight_history[None])
    act_q, peaks = activate(gate_pre, up_pre, weight_peak, act_history[None])
    blocks = share(grad_out, peaks, send(peaks, swap))
    blocks = [
        send(block, [(edge[0], edge[1]) for edge in ROUNDS[number]])
        for number, block in enumerate(blocks)
    ]
    grad, peaks = place(blocks)
    weight = stamp(weight_q, peaks)
    before, after = send(weight, feature_ring(1)), send(weight, feature_ring(-1))
    half = weight_q.shape[0] // 2
    weight, peaks = weight_tile(
        weight,
        after,
        send(before[:half], feature_ring(1)),
        send(after[half:], feature_ring(-1)),
        before,
    )
    peaks = jnp.maximum(peaks, send(peaks, swap))
    (act_q,) = gate((act_q,), (grad,))
    act = lax.all_gather(act_q, AXES, axis=0, tiled=True, axis_index_groups=groups)
    slope, silu, token = slopes(gate_pre, up_pre, (grad,))
    before, after = send(grad, hidden_ring(1)), send(grad, hidden_ring(-1))
    half = grad.shape[0] // 2
    tile = grad_tile(
        grad,
        after,
        send(before[:half], hidden_ring(1)),
        send(after[half:], hidden_ring(-1)),
        before,
        (token,),
    )

    def block_of(array, number):
        size = array.shape[1] // N
        return lax.dynamic_slice_in_dim(array, number % N * size, size, axis=1)

    grad_act = dot(tile, weight, ((1,), (1,)))
    grad_act = lax.psum_scatter(
        grad_act, AXES, scatter_dimension=0, tiled=True, axis_index_groups=groups
    )
    far = block_of(weight, z + 2)
    top = send(dot(act[:half], far, ((1,), (0,))), hidden_ring(1))
    bottom = send(dot(act[half:], far, ((1,), (0,))), hidden_ring(-1))
    mixed = [dot(act, block_of(weight, z + step), ((1,), (0,))) for step in (0, 1, 3)]
    (act,) = gate((act,), mixed)
    weight_grad = [
        dot(act, block_of(tile, feature_place + step), ((0,), (0,))) for step in range(N)
    ]
    after, before = add_halves(mixed[1], mixed[2], top, bottom, weight_grad)
    mixed = (mixed[0], send(after, hidden_ring(1)), send(before, hidden_ring(-1)))
    blocks = list(return_blocks(mixed, peaks))
    weight_grad, added = add(ring_exchange(weight_grad, feature_ring))
    grad_gate, grad_up, finished = finish(slope, silu, grad_act)
    blocks[2:] = gate(blocks[2:], (added, finished))
    blocks = [
        send(block, [(edge[1], edge[0]) for edge in ROUNDS[number]])
        for number, block in enumerate(blocks)
    ]
    mixed = merge(blocks, ())
    peaks = read_notes(blocks)
    new_weight, new_act = histories(
        peaks, send(peaks, swap), weight_history[None], act_history[None]
    )
    return (mixed, grad_gate, grad_up, weight_grad, new_weight[0], new_act[0])


def solution(mesh):
    cube = Mesh(mesh.devices.reshape(N, N, N, 2), AXES)
    whole = P(("x", "y"), ("z", "c"))
    flipped = P(("z", "c"), ("x", "y"))
    return jax.shard_map(
        on_device,
        mesh=cube,
        in_specs=(whole, whole, flipped, whole, P(), P()),
        out_specs=(whole, whole, whole, flipped, P(), P()),
        check_vma=False,
    )
```

```python
import functools

import jax
import jax.numpy as jnp
import numpy as np
from jax import lax
from jax.experimental import pallas as pl
from jax.experimental.pallas import tpu as pltpu
from jax.sharding import Mesh, PartitionSpec as P

AXES = ("x", "y", "z", "c")
N = 4
BF16 = jnp.bfloat16
F32 = jnp.float32
VMEM_BYTES = 24 * 1024 * 1024
ANYWHERE = pl.BlockSpec(memory_space=pl.ANY)
SCALARS = pl.BlockSpec(memory_space=pltpu.SMEM)
IN_VMEM = pl.BlockSpec(memory_space=pltpu.VMEM)
IN_HBM = pl.BlockSpec(memory_space=pltpu.HBM)
NOTE = 16


def flat(x, y, z, c):
    return ((x % N * N + y % N) * N + z % N) * 2 + c


def places():
    return [(x, y, z, c) for x in range(N) for y in range(N) for z in range(N) for c in range(2)]


def token_ring(step):
    return [
        (flat(x, y, z, c), flat(x, y + step, z, c) if c == 0 else flat(x + step, y, z, c))
        for x, y, z, c in places()
    ]


def feature_ring(step):
    return [
        (flat(x, y, z, c), flat(x + step, y, z, c) if c == 0 else flat(x, y + step, z, c))
        for x, y, z, c in places()
    ]


def hidden_ring(step):
    return [(flat(x, y, z, c), flat(x, y, z + step, c)) for x, y, z, c in places()]


def token_groups():
    first = [[flat(x, y, z, 0) for y in range(N)] for x in range(N) for z in range(N)]
    second = [[flat(x, y, z, 1) for x in range(N)] for y in range(N) for z in range(N)]
    return first + second


def tile_edges():
    edges = []
    for x, y, z, c in places():
        for half in range(2):
            block = 2 * c + half
            edges.append((flat(x, y, z, c), flat(x, block, z, 0), half, y))
            edges.append((flat(x, y, z, c), flat(z, y, block, 1), half, x))
    return edges


def rounds():
    rest = tile_edges()
    out = []
    for _ in range(4):
        outgoing = {}
        for edge in rest:
            outgoing.setdefault(edge[0], []).append(edge)
        chosen = {}

        def augment(owner, seen):
            for edge in outgoing[owner]:
                if edge[1] in seen:
                    continue
                seen.add(edge[1])
                if edge[1] not in chosen or augment(chosen[edge[1]][0], seen):
                    chosen[edge[1]] = edge
                    return True
            return False

        for owner in range(128):
            augment(owner, set())
        picked = sorted(chosen.values())
        out.append(picked)
        rest = [edge for edge in rest if edge not in picked]
    return out


ROUNDS = rounds()
TABLE = np.zeros((8, 128), np.int32)
for number, picked in enumerate(ROUNDS):
    for owner, user, half, slot in picked:
        TABLE[number, owner] = half
        TABLE[4 + number, user] = slot


def send(value, pairs):
    return lax.ppermute(value, AXES, pairs)


def here():
    x, y, z, c = (lax.axis_index(name) for name in AXES)
    return flat(x, y, z, c), jnp.where(c == 0, x, y), z


def call(kernel, out_shape, cost, in_specs, operands, after=(), stored=(), vmem=VMEM_BYTES, **options):
    flops, moved = cost
    count = len(operands)
    extra = len(after) + len(stored)

    def body(*refs):
        kernel(*refs[:count], *refs[count + extra :])

    return pl.pallas_call(
        body,
        out_shape=out_shape,
        in_specs=list(in_specs) + [ANYWHERE] * len(after) + [IN_HBM] * len(stored),
        compiler_params=pltpu.CompilerParams(vmem_limit_bytes=vmem),
        cost_estimate=pl.CostEstimate(flops=flops, bytes_accessed=moved, transcendentals=0),
        **options,
    )(*operands, *after, *stored)


def shape(*dims, dtype=BF16):
    return jax.ShapeDtypeStruct(dims, dtype)


def ring_gather(own, ring):
    far = send(own, ring(2))
    return own, send(own, ring(-1)), far, send(own, ring(1))


def ring_exchange(parts, ring):
    far = send(parts[2], ring(2))
    return parts[0], send(parts[1], ring(1)), far, send(parts[3], ring(-1))


def peak_of(values):
    return jnp.max(jnp.abs(values), axis=0, keepdims=True)


def keep_peak(step, top, peak):
    @pl.when(step == 0)
    def _():
        top[...] = peak

    @pl.when(step > 0)
    def _():
        top[...] = jnp.maximum(top[...], peak)


def row_blocks(array, steps):
    return pl.BlockSpec((array.shape[0] // steps, array.shape[1]), lambda i: (i, 0))


def fixed(*dims):
    return pl.BlockSpec(dims, lambda i: (0, 0))


def note_of(peaks, width):
    row = lax.broadcasted_iota(jnp.int32, (NOTE, width), 0)
    note = jnp.zeros((NOTE, width), F32)
    for number in range(2):
        rest = jnp.broadcast_to(peaks[number : number + 1, :1], (NOTE, width))
        for piece in range(3):
            value = rest.astype(BF16).astype(F32)
            note = jnp.where(row == 3 * number + piece, value, note)
            rest = rest - value
    return note.astype(BF16)


def peaks_in(notes):
    best = []
    for number in range(2):
        values = []
        for note in notes:
            note = note[...].astype(F32)
            pieces = [note[3 * number + piece : 3 * number + piece + 1, :128] for piece in range(3)]
            values.append(pieces[0] + pieces[1] + pieces[2])
        best.append(functools.reduce(jnp.maximum, values))
    row = lax.broadcasted_iota(jnp.int32, (8, 128), 0)
    return jnp.where(row == 0, jnp.broadcast_to(best[0], (8, 128)), jnp.broadcast_to(best[1], (8, 128)))


def note_block(array):
    last = array.shape[0] // NOTE - 1
    return pl.BlockSpec((NOTE, array.shape[1]), lambda *i: (last, 0))


def share_kernel(table, grad, peaks, others, out0, out1, out2, out3):
    me, _, _ = here()
    tokens, width = grad.shape[0], grad.shape[1] // 2
    note = note_of(jnp.maximum(peaks[...], others[...]), width)
    for number, out in enumerate((out0, out1, out2, out3)):
        half = table[number, me]

        @pl.when(half == 0)
        def _():
            out[:tokens, :] = grad[:, :width]

        @pl.when(half == 1)
        def _():
            out[:tokens, :] = grad[:, width:]

        out[tokens:, :] = note


def share(grad, peaks, others):
    block = shape(grad.shape[0] + NOTE, grad.shape[1] // 2)
    return call(
        share_kernel,
        (block, block, block, block),
        (0, 0),
        [SCALARS] + [IN_VMEM] * 3,
        (jnp.asarray(TABLE), grad, peaks, others),
        out_specs=[IN_VMEM] * 4,
    )


def clip_kernel(weight, history, weight_q, peak, top):
    step = pl.program_id(0)
    weight_v = weight[...].astype(F32)
    limit = jnp.max(history[...], axis=1, keepdims=True)
    weight_q[...] = jnp.clip(weight_v, -limit, limit).astype(BF16)
    keep_peak(step, top, peak_of(weight_v))

    @pl.when(step == pl.num_programs(0) - 1)
    def _():
        peak[...] = jnp.broadcast_to(jnp.max(top[...], axis=1, keepdims=True), peak.shape)


def clip_weight(weight, history):
    steps = 2
    rows = row_blocks(weight, steps)
    return call(
        clip_kernel,
        (shape(*weight.shape), shape(8, 128, dtype=F32)),
        (0, 0),
        [rows, fixed(1, history.shape[1])],
        (weight, history),
        grid=(steps,),
        out_specs=[rows, fixed(8, 128)],
        scratch_shapes=[pltpu.VMEM((1, weight.shape[1]), F32)],
    )


def activate_kernel(gate, up, weight_peak, history, act_q, peaks, top):
    step = pl.program_id(0)
    gate_v = gate[...].astype(F32)
    act = gate_v * jax.nn.sigmoid(gate_v) * up[...].astype(F32)
    limit = jnp.max(history[...], axis=1, keepdims=True)
    act_q[...] = jnp.clip(act, -limit, limit).astype(BF16)
    keep_peak(step, top, peak_of(act))

    @pl.when(step == pl.num_programs(0) - 1)
    def _():
        row = lax.broadcasted_iota(jnp.int32, peaks.shape, 0)
        act_peak = jnp.broadcast_to(jnp.max(top[...], axis=1, keepdims=True), peaks.shape)
        peaks[...] = jnp.where(row == 0, act_peak, weight_peak[...])


def activate(gate, up, weight_peak, history):
    steps = 8
    rows = row_blocks(gate, steps)
    return call(
        activate_kernel,
        (shape(*gate.shape), shape(8, 128, dtype=F32)),
        (0, 0),
        [rows, rows, fixed(8, 128), fixed(1, history.shape[1])],
        (gate, up, weight_peak, history),
        grid=(steps,),
        out_specs=[rows, fixed(8, 128)],
        scratch_shapes=[pltpu.VMEM((1, gate.shape[1]), F32)],
    )


def slopes_kernel(gate, up, slope, silu, token):
    gate_v = gate[...].astype(F32)
    sigm = jax.nn.sigmoid(gate_v)
    slope[...] = (up[...].astype(F32) * sigm * (1.0 + gate_v * (1.0 - sigm))).astype(BF16)
    silu[...] = (gate_v * sigm).astype(BF16)
    token[...] = jnp.zeros(token.shape, F32)


def slopes(gate, up, after):
    steps = 8
    rows = row_blocks(gate, steps)
    return call(
        slopes_kernel,
        (shape(*gate.shape), shape(*gate.shape), shape(8, 128, dtype=F32)),
        (0, 0),
        [rows, rows],
        (gate, up),
        after,
        grid=(steps,),
        out_specs=[rows, rows, fixed(8, 128)],
    )


def place_kernel(table, in0, in1, in2, in3, out, peaks):
    me, _, _ = here()
    rows = in0.shape[0] - NOTE
    for number, block in enumerate((in0, in1, in2, in3)):
        start = pl.multiple_of(table[4 + number, me] * rows, rows)
        out[pl.ds(start, rows), :] = block[:rows, :]
    peaks[...] = peaks_in([block[rows:, :] for block in (in0, in1, in2, in3)])


def place(blocks):
    rows, features = blocks[0].shape
    return call(
        place_kernel,
        (shape(4 * (rows - NOTE), features), shape(8, 128, dtype=F32)),
        (0, 0),
        [SCALARS] + [IN_VMEM] * 4,
        (jnp.asarray(TABLE), *blocks),
        out_specs=[IN_VMEM] * 2,
    )


def stamp_kernel(weight, peaks, out):
    rows = weight.shape[0]
    out[:rows, :] = weight[...]
    out[rows:, :] = note_of(peaks[...], weight.shape[1])


def stamp(weight, peaks):
    return call(
        stamp_kernel,
        shape(weight.shape[0] + NOTE, weight.shape[1]),
        (0, 0),
        [IN_VMEM] * 2,
        (weight, peaks),
        out_specs=IN_VMEM,
    )


def gate_kernel(*refs):
    pass


def gate(values, after=(), stored=()):
    count = len(values)
    return call(
        gate_kernel,
        tuple(shape(*value.shape) for value in values),
        (0, 0),
        [ANYWHERE] * count,
        values,
        after,
        stored,
        vmem=1024 * 1024,
        out_specs=[ANYWHERE] * count,
        input_output_aliases={number: number for number in range(count)},
    )


def columns_kernel(place, own, after, far, before, out):
    width = own.shape[1]
    for step, block in enumerate((own, after, far, before)):
        column = (place + step) % N * width
        if not isinstance(column, int):
            column = pl.multiple_of(column, width)
        out[:, pl.ds(column, width)] = block[...]


def half_blocks(steps, dims):
    first = pl.BlockSpec(dims, lambda i: (jnp.minimum(i, steps // 2 - 1), 0))
    second = pl.BlockSpec(dims, lambda i: (jnp.maximum(i - steps // 2, 0), 0))
    return [first, second]


def weight_tile_kernel(own, after, top, bottom, before, note0, note1, note2, note3, out, peaks):
    place = here()[1]
    step = pl.program_id(0)

    @pl.when(step < pl.num_programs(0) // 2)
    def _():
        columns_kernel(place, own, after, top, before, out)

    @pl.when(step >= pl.num_programs(0) // 2)
    def _():
        columns_kernel(place, own, after, bottom, before, out)

    peaks[...] = peaks_in((note0, note1, note2, note3))


def weight_tile(own, after, top, bottom, before):
    steps = 4
    hidden, features = own.shape[0] - NOTE, own.shape[1]
    dims = (hidden // steps, features)
    block = pl.BlockSpec(dims, lambda i: (i, 0))
    out = shape(hidden, N * features)
    noted = (own, after, bottom, before)
    return call(
        weight_tile_kernel,
        (out, shape(8, 128, dtype=F32)),
        (0, 0),
        [block, block, *half_blocks(steps, dims), block] + [note_block(part) for part in noted],
        (own, after, top, bottom, before, *noted),
        grid=(steps,),
        out_specs=[row_blocks(out, steps), fixed(8, 128)],
    )


def raise_kernel(after, before, top, bottom, out_after, out_before):
    rows = top.shape[0]
    out_after[:rows, :] = (after[:rows, :].astype(F32) + top[...].astype(F32)).astype(BF16)
    out_after[rows:, :] = after[rows:, :]
    out_before[:rows, :] = before[:rows, :]
    out_before[rows:, :] = (before[rows:, :].astype(F32) + bottom[...].astype(F32)).astype(BF16)


def add_halves(after, before, top, bottom, order):
    whole = shape(*after.shape)
    return call(
        raise_kernel,
        (whole, whole),
        (0, 0),
        [IN_VMEM] * 4,
        (after, before, top, bottom),
        order,
        out_specs=[IN_VMEM] * 2,
    )


def grad_tile_kernel(own, after, top, bottom, before, out):
    place = here()[2]
    step = pl.program_id(0)

    @pl.when(step < pl.num_programs(0) // 2)
    def _():
        columns_kernel(place, own, after, top, before, out)

    @pl.when(step >= pl.num_programs(0) // 2)
    def _():
        columns_kernel(place, own, after, bottom, before, out)


def grad_tile(own, after, top, bottom, before, order):
    steps = 4
    rows, features = own.shape
    dims = (rows // steps, features)
    block = pl.BlockSpec(dims, lambda i: (i, 0))
    out = shape(rows, N * features)
    return call(
        grad_tile_kernel,
        out,
        (0, 0),
        [block, block, *half_blocks(steps, dims), block],
        (own, after, top, bottom, before),
        order,
        grid=(steps,),
        out_specs=row_blocks(out, steps),
    )


def histories_kernel(peaks, others, old_weight, old_act, new_weight, new_act):
    for row, old, new in ((1, old_weight, new_weight), (0, old_act, new_act)):
        new[:, 1:] = old[:, :-1]
        new[:, :1] = jnp.maximum(peaks[row : row + 1, :1], others[row : row + 1, :1])


def histories(peaks, others, old_weight, old_act):
    new = shape(*old_weight.shape, dtype=F32)
    return call(
        histories_kernel,
        (new, new),
        (0, 0),
        [IN_VMEM] * 4,
        (peaks, others, old_weight, old_act),
        out_specs=[IN_VMEM] * 2,
    )


def return_kernel(table, own, before, after, peaks, out0, out1, out2, out3):
    me, _, _ = here()
    tokens = out0.shape[0] - NOTE
    note = note_of(peaks[...], out0.shape[1])
    for number, out in enumerate((out0, out1, out2, out3)):
        rows = pl.ds(pl.multiple_of(table[4 + number, me] * tokens, tokens), tokens)
        total = own[rows, :].astype(F32) + before[rows, :].astype(F32) + after[rows, :].astype(F32)
        out[:tokens, :] = total.astype(BF16)
        out[tokens:, :] = note


def return_blocks(parts, peaks):
    rows, features = parts[0].shape
    return call(
        return_kernel,
        (shape(rows // N + NOTE, features),) * 4,
        (0, 0),
        [SCALARS] + [IN_VMEM] * 4,
        (jnp.asarray(TABLE), *parts, peaks),
        out_specs=[IN_VMEM] * 4,
    )


def read_kernel(note0, note1, note2, note3, peaks):
    peaks[...] = peaks_in((note0, note1, note2, note3))


def read_notes(blocks):
    return call(
        read_kernel,
        shape(8, 128, dtype=F32),
        (0, 0),
        [note_block(block) for block in blocks],
        blocks,
        grid=(1,),
        out_specs=fixed(8, 128),
    )


def add_kernel(part0, part1, part2, part3, out, token):
    total = part0[...].astype(F32) + part1[...].astype(F32)
    out[...] = (total + (part2[...].astype(F32) + part3[...].astype(F32))).astype(BF16)
    token[...] = jnp.zeros(token.shape, F32)


def add(parts, after):
    steps = 4
    rows = row_blocks(parts[0], steps)
    return call(
        add_kernel,
        (shape(*parts[0].shape), shape(8, 128, dtype=F32)),
        (0, 0),
        [rows] * 4,
        parts,
        after,
        grid=(steps,),
        out_specs=[rows, fixed(8, 128)],
    )


def merge_kernel(table, in0, in1, in2, in3, out):
    me, _, _ = here()
    width = in0.shape[1]
    for half in range(2):
        total = jnp.zeros(in0.shape, F32)
        for number, block in enumerate((in0, in1, in2, in3)):
            keep = (table[number, me] == half).astype(F32)
            total = total + block[...].astype(F32) * keep
        out[:, half * width : (half + 1) * width] = total.astype(BF16)


def merge(blocks, after):
    steps = 2
    tokens, features = blocks[0].shape[0] - NOTE, blocks[0].shape[1]
    block = pl.BlockSpec((tokens // steps, features), lambda i: (i, 0))
    out = shape(tokens, 2 * features)
    return call(
        merge_kernel,
        out,
        (0, 0),
        [SCALARS] + [block] * 4,
        (jnp.asarray(TABLE), *blocks),
        after,
        grid=(steps,),
        out_specs=row_blocks(out, steps),
    )


def finish_kernel(slope, silu, grad_act, grad_gate, grad_up, token):
    value = grad_act[...].astype(F32)
    grad_gate[...] = (value * slope[...].astype(F32)).astype(BF16)
    grad_up[...] = (value * silu[...].astype(F32)).astype(BF16)
    token[...] = jnp.zeros(token.shape, F32)


def finish(slope, silu, grad_act):
    steps = 4
    rows = row_blocks(slope, steps)
    return call(
        finish_kernel,
        (shape(*slope.shape), shape(*slope.shape), shape(8, 128, dtype=F32)),
        (0, 0),
        [rows] * 3,
        (slope, silu, grad_act),
        grid=(steps,),
        out_specs=[rows, rows, fixed(8, 128)],
    )


def dot(left, right, dims):
    product = lax.dot_general(left, right, (dims, ((), ())), preferred_element_type=F32)
    return product.astype(BF16)


def on_device(gate_pre, up_pre, down_weight, grad_out, weight_history, act_history):
    _, feature_place, z = here()
    groups = token_groups()
    swap = [(n, n ^ 1) for n in range(128)]
    weight_q, weight_peak = clip_weight(down_weight, weight_history[None])
    act_q, peaks = activate(gate_pre, up_pre, weight_peak, act_history[None])
    blocks = share(grad_out, peaks, send(peaks, swap))
    blocks = [
        send(block, [(edge[0], edge[1]) for edge in ROUNDS[number]])
        for number, block in enumerate(blocks)
    ]
    grad, peaks = place(blocks)
    weight = stamp(weight_q, peaks)
    before, after = send(weight, feature_ring(1)), send(weight, feature_ring(-1))
    half = weight_q.shape[0] // 2
    weight, peaks = weight_tile(
        weight,
        after,
        send(before[:half], feature_ring(1)),
        send(after[half:], feature_ring(-1)),
        before,
    )
    peaks = jnp.maximum(peaks, send(peaks, swap))
    (act_q,) = gate((act_q,), (grad,))
    act = lax.all_gather(act_q, AXES, axis=0, tiled=True, axis_index_groups=groups)
    slope, silu, token = slopes(gate_pre, up_pre, (grad,))
    before, after = send(grad, hidden_ring(1)), send(grad, hidden_ring(-1))
    half = grad.shape[0] // 2
    tile = grad_tile(
        grad,
        after,
        send(before[:half], hidden_ring(1)),
        send(after[half:], hidden_ring(-1)),
        before,
        (token,),
    )

    def block_of(array, number):
        size = array.shape[1] // N
        return lax.dynamic_slice_in_dim(array, number % N * size, size, axis=1)

    grad_act = dot(tile, weight, ((1,), (1,)))
    grad_act = lax.psum_scatter(
        grad_act, AXES, scatter_dimension=0, tiled=True, axis_index_groups=groups
    )
    far = block_of(weight, z + 2)
    top = send(dot(act[:half], far, ((1,), (0,))), hidden_ring(1))
    bottom = send(dot(act[half:], far, ((1,), (0,))), hidden_ring(-1))
    mixed = [dot(act, block_of(weight, z + step), ((1,), (0,))) for step in (0, 1, 3)]
    (act,) = gate((act,), mixed)
    weight_grad = [
        dot(act, block_of(tile, feature_place + step), ((0,), (0,))) for step in range(N)
    ]
    after, before = add_halves(mixed[1], mixed[2], top, bottom, weight_grad[2:])
    mixed = (mixed[0], send(after, hidden_ring(1)), send(before, hidden_ring(-1)))
    blocks = list(return_blocks(mixed, peaks))
    weight_grad, added = add(ring_exchange(weight_grad, feature_ring), blocks[:1])
    grad_gate, grad_up, finished = finish(slope, silu, grad_act)
    blocks[2:] = gate(blocks[2:], (added, finished))
    blocks = [
        send(block, [(edge[1], edge[0]) for edge in ROUNDS[number]])
        for number, block in enumerate(blocks)
    ]
    mixed = merge(blocks, ())
    peaks = read_notes(blocks)
    new_weight, new_act = histories(
        peaks, send(peaks, swap), weight_history[None], act_history[None]
    )
    return (mixed, grad_gate, grad_up, weight_grad, new_weight[0], new_act[0])


def solution(mesh):
    cube = Mesh(mesh.devices.reshape(N, N, N, 2), AXES)
    whole = P(("x", "y"), ("z", "c"))
    flipped = P(("z", "c"), ("x", "y"))
    return jax.shard_map(
        on_device,
        mesh=cube,
        in_specs=(whole, whole, flipped, whole, P(), P()),
        out_specs=(whole, whole, whole, flipped, P(), P()),
        check_vma=False,
    )
```

```python
import functools

import jax
import jax.numpy as jnp
import numpy as np
from jax import lax
from jax.experimental import pallas as pl
from jax.experimental.pallas import tpu as pltpu
from jax.sharding import Mesh, PartitionSpec as P

AXES = ("x", "y", "z", "c")
N = 4
BF16 = jnp.bfloat16
F32 = jnp.float32
VMEM_BYTES = 24 * 1024 * 1024
ANYWHERE = pl.BlockSpec(memory_space=pl.ANY)
SCALARS = pl.BlockSpec(memory_space=pltpu.SMEM)
IN_VMEM = pl.BlockSpec(memory_space=pltpu.VMEM)
IN_HBM = pl.BlockSpec(memory_space=pltpu.HBM)
NOTE = 16


def flat(x, y, z, c):
    return ((x % N * N + y % N) * N + z % N) * 2 + c


def places():
    return [(x, y, z, c) for x in range(N) for y in range(N) for z in range(N) for c in range(2)]


def token_ring(step):
    return [
        (flat(x, y, z, c), flat(x, y + step, z, c) if c == 0 else flat(x + step, y, z, c))
        for x, y, z, c in places()
    ]


def feature_ring(step):
    return [
        (flat(x, y, z, c), flat(x + step, y, z, c) if c == 0 else flat(x, y + step, z, c))
        for x, y, z, c in places()
    ]


def hidden_ring(step):
    return [(flat(x, y, z, c), flat(x, y, z + step, c)) for x, y, z, c in places()]


def token_groups():
    first = [[flat(x, y, z, 0) for y in range(N)] for x in range(N) for z in range(N)]
    second = [[flat(x, y, z, 1) for x in range(N)] for y in range(N) for z in range(N)]
    return first + second


def tile_edges():
    edges = []
    for x, y, z, c in places():
        for half in range(2):
            block = 2 * c + half
            edges.append((flat(x, y, z, c), flat(x, block, z, 0), half, y))
            edges.append((flat(x, y, z, c), flat(z, y, block, 1), half, x))
    return edges


def rounds():
    rest = tile_edges()
    out = []
    for _ in range(4):
        outgoing = {}
        for edge in rest:
            outgoing.setdefault(edge[0], []).append(edge)
        chosen = {}

        def augment(owner, seen):
            for edge in outgoing[owner]:
                if edge[1] in seen:
                    continue
                seen.add(edge[1])
                if edge[1] not in chosen or augment(chosen[edge[1]][0], seen):
                    chosen[edge[1]] = edge
                    return True
            return False

        for owner in range(128):
            augment(owner, set())
        picked = sorted(chosen.values())
        out.append(picked)
        rest = [edge for edge in rest if edge not in picked]
    return out


ROUNDS = rounds()
TABLE = np.zeros((8, 128), np.int32)
for number, picked in enumerate(ROUNDS):
    for owner, user, half, slot in picked:
        TABLE[number, owner] = half
        TABLE[4 + number, user] = slot


def send(value, pairs):
    return lax.ppermute(value, AXES, pairs)


def here():
    x, y, z, c = (lax.axis_index(name) for name in AXES)
    return flat(x, y, z, c), jnp.where(c == 0, x, y), z


def call(kernel, out_shape, cost, in_specs, operands, after=(), stored=(), vmem=VMEM_BYTES, **options):
    flops, moved = cost
    count = len(operands)
    extra = len(after) + len(stored)

    def body(*refs):
        kernel(*refs[:count], *refs[count + extra :])

    return pl.pallas_call(
        body,
        out_shape=out_shape,
        in_specs=list(in_specs) + [ANYWHERE] * len(after) + [IN_HBM] * len(stored),
        compiler_params=pltpu.CompilerParams(vmem_limit_bytes=vmem),
        cost_estimate=pl.CostEstimate(flops=flops, bytes_accessed=moved, transcendentals=0),
        **options,
    )(*operands, *after, *stored)


def shape(*dims, dtype=BF16):
    return jax.ShapeDtypeStruct(dims, dtype)


def ring_gather(own, ring):
    far = send(own, ring(2))
    return own, send(own, ring(-1)), far, send(own, ring(1))


def ring_exchange(parts, ring):
    far = send(parts[2], ring(2))
    return parts[0], send(parts[1], ring(1)), far, send(parts[3], ring(-1))


def peak_of(values):
    return jnp.max(jnp.abs(values), axis=0, keepdims=True)


def keep_peak(step, top, peak):
    @pl.when(step == 0)
    def _():
        top[...] = peak

    @pl.when(step > 0)
    def _():
        top[...] = jnp.maximum(top[...], peak)


def row_blocks(array, steps):
    return pl.BlockSpec((array.shape[0] // steps, array.shape[1]), lambda i: (i, 0))


def fixed(*dims):
    return pl.BlockSpec(dims, lambda i: (0, 0))


def note_of(peaks, width):
    row = lax.broadcasted_iota(jnp.int32, (NOTE, width), 0)
    note = jnp.zeros((NOTE, width), F32)
    for number in range(2):
        rest = jnp.broadcast_to(peaks[number : number + 1, :1], (NOTE, width))
        for piece in range(3):
            value = rest.astype(BF16).astype(F32)
            note = jnp.where(row == 3 * number + piece, value, note)
            rest = rest - value
    return note.astype(BF16)


def peaks_in(notes):
    best = []
    for number in range(2):
        values = []
        for note in notes:
            note = note[...].astype(F32)
            pieces = [note[3 * number + piece : 3 * number + piece + 1, :128] for piece in range(3)]
            values.append(pieces[0] + pieces[1] + pieces[2])
        best.append(functools.reduce(jnp.maximum, values))
    row = lax.broadcasted_iota(jnp.int32, (8, 128), 0)
    return jnp.where(row == 0, jnp.broadcast_to(best[0], (8, 128)), jnp.broadcast_to(best[1], (8, 128)))


def note_block(array):
    last = array.shape[0] // NOTE - 1
    return pl.BlockSpec((NOTE, array.shape[1]), lambda *i: (last, 0))


def share_kernel(table, grad, peaks, others, out0, out1, out2, out3):
    me, _, _ = here()
    tokens, width = grad.shape[0], grad.shape[1] // 2
    note = note_of(jnp.maximum(peaks[...], others[...]), width)
    for number, out in enumerate((out0, out1, out2, out3)):
        half = table[number, me]

        @pl.when(half == 0)
        def _():
            out[:tokens, :] = grad[:, :width]

        @pl.when(half == 1)
        def _():
            out[:tokens, :] = grad[:, width:]

        out[tokens:, :] = note


def share(grad, peaks, others):
    block = shape(grad.shape[0] + NOTE, grad.shape[1] // 2)
    return call(
        share_kernel,
        (block, block, block, block),
        (0, 0),
        [SCALARS] + [IN_VMEM] * 3,
        (jnp.asarray(TABLE), grad, peaks, others),
        out_specs=[IN_VMEM] * 4,
    )


def clip_kernel(weight, history, weight_q, peak, top):
    step = pl.program_id(0)
    weight_v = weight[...].astype(F32)
    limit = jnp.max(history[...], axis=1, keepdims=True)
    weight_q[...] = jnp.clip(weight_v, -limit, limit).astype(BF16)
    keep_peak(step, top, peak_of(weight_v))

    @pl.when(step == pl.num_programs(0) - 1)
    def _():
        peak[...] = jnp.broadcast_to(jnp.max(top[...], axis=1, keepdims=True), peak.shape)


def clip_weight(weight, history):
    steps = 2
    rows = row_blocks(weight, steps)
    return call(
        clip_kernel,
        (shape(*weight.shape), shape(8, 128, dtype=F32)),
        (0, 0),
        [rows, fixed(1, history.shape[1])],
        (weight, history),
        grid=(steps,),
        out_specs=[rows, fixed(8, 128)],
        scratch_shapes=[pltpu.VMEM((1, weight.shape[1]), F32)],
    )


def activate_kernel(gate, up, weight_peak, history, act_q, peaks, top):
    step = pl.program_id(0)
    gate_v = gate[...].astype(F32)
    act = gate_v * jax.nn.sigmoid(gate_v) * up[...].astype(F32)
    limit = jnp.max(history[...], axis=1, keepdims=True)
    act_q[...] = jnp.clip(act, -limit, limit).astype(BF16)
    keep_peak(step, top, peak_of(act))

    @pl.when(step == pl.num_programs(0) - 1)
    def _():
        row = lax.broadcasted_iota(jnp.int32, peaks.shape, 0)
        act_peak = jnp.broadcast_to(jnp.max(top[...], axis=1, keepdims=True), peaks.shape)
        peaks[...] = jnp.where(row == 0, act_peak, weight_peak[...])


def activate(gate, up, weight_peak, history):
    steps = 8
    rows = row_blocks(gate, steps)
    return call(
        activate_kernel,
        (shape(*gate.shape), shape(8, 128, dtype=F32)),
        (0, 0),
        [rows, rows, fixed(8, 128), fixed(1, history.shape[1])],
        (gate, up, weight_peak, history),
        grid=(steps,),
        out_specs=[rows, fixed(8, 128)],
        scratch_shapes=[pltpu.VMEM((1, gate.shape[1]), F32)],
    )


def slopes_kernel(gate, up, slope, silu, token):
    gate_v = gate[...].astype(F32)
    sigm = jax.nn.sigmoid(gate_v)
    slope[...] = (up[...].astype(F32) * sigm * (1.0 + gate_v * (1.0 - sigm))).astype(BF16)
    silu[...] = (gate_v * sigm).astype(BF16)
    token[...] = jnp.zeros(token.shape, F32)


def slopes(gate, up, after):
    steps = 8
    rows = row_blocks(gate, steps)
    return call(
        slopes_kernel,
        (shape(*gate.shape), shape(*gate.shape), shape(8, 128, dtype=F32)),
        (0, 0),
        [rows, rows],
        (gate, up),
        after,
        grid=(steps,),
        out_specs=[rows, rows, fixed(8, 128)],
    )


def place_kernel(table, in0, in1, in2, in3, out, peaks):
    me, _, _ = here()
    rows = in0.shape[0] - NOTE
    for number, block in enumerate((in0, in1, in2, in3)):
        start = pl.multiple_of(table[4 + number, me] * rows, rows)
        out[pl.ds(start, rows), :] = block[:rows, :]
    peaks[...] = peaks_in([block[rows:, :] for block in (in0, in1, in2, in3)])


def place(blocks):
    rows, features = blocks[0].shape
    return call(
        place_kernel,
        (shape(4 * (rows - NOTE), features), shape(8, 128, dtype=F32)),
        (0, 0),
        [SCALARS] + [IN_VMEM] * 4,
        (jnp.asarray(TABLE), *blocks),
        out_specs=[IN_VMEM] * 2,
    )


def stamp_kernel(weight, peaks, out):
    rows = weight.shape[0]
    out[:rows, :] = weight[...]
    out[rows:, :] = note_of(peaks[...], weight.shape[1])


def stamp(weight, peaks):
    return call(
        stamp_kernel,
        shape(weight.shape[0] + NOTE, weight.shape[1]),
        (0, 0),
        [IN_VMEM] * 2,
        (weight, peaks),
        out_specs=IN_VMEM,
    )


def gate_kernel(*refs):
    pass


def gate(values, after=(), stored=()):
    count = len(values)
    return call(
        gate_kernel,
        tuple(shape(*value.shape) for value in values),
        (0, 0),
        [ANYWHERE] * count,
        values,
        after,
        stored,
        vmem=1024 * 1024,
        out_specs=[ANYWHERE] * count,
        input_output_aliases={number: number for number in range(count)},
    )


def columns_kernel(place, own, after, far, before, out):
    width = own.shape[1]
    for step, block in enumerate((own, after, far, before)):
        column = (place + step) % N * width
        if not isinstance(column, int):
            column = pl.multiple_of(column, width)
        out[:, pl.ds(column, width)] = block[...]


def half_blocks(steps, dims):
    first = pl.BlockSpec(dims, lambda i: (jnp.minimum(i, steps // 2 - 1), 0))
    second = pl.BlockSpec(dims, lambda i: (jnp.maximum(i - steps // 2, 0), 0))
    return [first, second]


def weight_tile_kernel(own, after, top, bottom, before, note0, note1, note2, note3, out, peaks):
    place = here()[1]
    step = pl.program_id(0)

    @pl.when(step < pl.num_programs(0) // 2)
    def _():
        columns_kernel(place, own, after, top, before, out)

    @pl.when(step >= pl.num_programs(0) // 2)
    def _():
        columns_kernel(place, own, after, bottom, before, out)

    peaks[...] = peaks_in((note0, note1, note2, note3))


def weight_tile(own, after, top, bottom, before):
    steps = 4
    hidden, features = own.shape[0] - NOTE, own.shape[1]
    dims = (hidden // steps, features)
    block = pl.BlockSpec(dims, lambda i: (i, 0))
    out = shape(hidden, N * features)
    noted = (own, after, bottom, before)
    return call(
        weight_tile_kernel,
        (out, shape(8, 128, dtype=F32)),
        (0, 0),
        [block, block, *half_blocks(steps, dims), block] + [note_block(part) for part in noted],
        (own, after, top, bottom, before, *noted),
        grid=(steps,),
        out_specs=[row_blocks(out, steps), fixed(8, 128)],
    )


def raise_kernel(after, before, top, bottom, out_after, out_before):
    rows = top.shape[0]
    out_after[:rows, :] = (after[:rows, :].astype(F32) + top[...].astype(F32)).astype(BF16)
    out_after[rows:, :] = after[rows:, :]
    out_before[:rows, :] = before[:rows, :]
    out_before[rows:, :] = (before[rows:, :].astype(F32) + bottom[...].astype(F32)).astype(BF16)


def add_halves(after, before, top, bottom, order):
    whole = shape(*after.shape)
    return call(
        raise_kernel,
        (whole, whole),
        (0, 0),
        [IN_VMEM] * 4,
        (after, before, top, bottom),
        order,
        out_specs=[IN_VMEM] * 2,
    )


def grad_tile_kernel(own, after, top, bottom, before, out):
    place = here()[2]
    step = pl.program_id(0)

    @pl.when(step < pl.num_programs(0) // 2)
    def _():
        columns_kernel(place, own, after, top, before, out)

    @pl.when(step >= pl.num_programs(0) // 2)
    def _():
        columns_kernel(place, own, after, bottom, before, out)


def grad_tile(own, after, top, bottom, before, order):
    steps = 4
    rows, features = own.shape
    dims = (rows // steps, features)
    block = pl.BlockSpec(dims, lambda i: (i, 0))
    out = shape(rows, N * features)
    return call(
        grad_tile_kernel,
        out,
        (0, 0),
        [block, block, *half_blocks(steps, dims), block],
        (own, after, top, bottom, before),
        order,
        grid=(steps,),
        out_specs=row_blocks(out, steps),
    )


def histories_kernel(peaks, others, old_weight, old_act, new_weight, new_act):
    for row, old, new in ((1, old_weight, new_weight), (0, old_act, new_act)):
        new[:, 1:] = old[:, :-1]
        new[:, :1] = jnp.maximum(peaks[row : row + 1, :1], others[row : row + 1, :1])


def histories(peaks, others, old_weight, old_act):
    new = shape(*old_weight.shape, dtype=F32)
    return call(
        histories_kernel,
        (new, new),
        (0, 0),
        [IN_VMEM] * 4,
        (peaks, others, old_weight, old_act),
        out_specs=[IN_VMEM] * 2,
    )


def return_kernel(table, own, before, after, peaks, out0, out1, out2, out3):
    me, _, _ = here()
    tokens = out0.shape[0] - NOTE
    note = note_of(peaks[...], out0.shape[1])
    for number, out in enumerate((out0, out1, out2, out3)):
        rows = pl.ds(pl.multiple_of(table[4 + number, me] * tokens, tokens), tokens)
        total = own[rows, :].astype(F32) + before[rows, :].astype(F32) + after[rows, :].astype(F32)
        out[:tokens, :] = total.astype(BF16)
        out[tokens:, :] = note


def return_blocks(parts, peaks):
    rows, features = parts[0].shape
    return call(
        return_kernel,
        (shape(rows // N + NOTE, features),) * 4,
        (0, 0),
        [SCALARS] + [IN_VMEM] * 4,
        (jnp.asarray(TABLE), *parts, peaks),
        out_specs=[IN_VMEM] * 4,
    )


def read_kernel(note0, note1, note2, note3, peaks):
    peaks[...] = peaks_in((note0, note1, note2, note3))


def read_notes(blocks):
    return call(
        read_kernel,
        shape(8, 128, dtype=F32),
        (0, 0),
        [note_block(block) for block in blocks],
        blocks,
        grid=(1,),
        out_specs=fixed(8, 128),
    )


def add_kernel(part0, part1, part2, part3, out, token):
    total = part0[...].astype(F32) + part1[...].astype(F32)
    out[...] = (total + (part2[...].astype(F32) + part3[...].astype(F32))).astype(BF16)
    token[...] = jnp.zeros(token.shape, F32)


def add(parts, after):
    steps = 4
    rows = row_blocks(parts[0], steps)
    return call(
        add_kernel,
        (shape(*parts[0].shape), shape(8, 128, dtype=F32)),
        (0, 0),
        [rows] * 4,
        parts,
        after,
        grid=(steps,),
        out_specs=[rows, fixed(8, 128)],
    )


def merge_kernel(table, in0, in1, in2, in3, out):
    me, _, _ = here()
    width = in0.shape[1]
    for half in range(2):
        total = jnp.zeros(in0.shape, F32)
        for number, block in enumerate((in0, in1, in2, in3)):
            keep = (table[number, me] == half).astype(F32)
            total = total + block[...].astype(F32) * keep
        out[:, half * width : (half + 1) * width] = total.astype(BF16)


def merge(blocks, after):
    steps = 2
    tokens, features = blocks[0].shape[0] - NOTE, blocks[0].shape[1]
    block = pl.BlockSpec((tokens // steps, features), lambda i: (i, 0))
    out = shape(tokens, 2 * features)
    return call(
        merge_kernel,
        out,
        (0, 0),
        [SCALARS] + [block] * 4,
        (jnp.asarray(TABLE), *blocks),
        after,
        grid=(steps,),
        out_specs=row_blocks(out, steps),
    )


def finish_kernel(slope, silu, grad_act, grad_gate, grad_up, token):
    value = grad_act[...].astype(F32)
    grad_gate[...] = (value * slope[...].astype(F32)).astype(BF16)
    grad_up[...] = (value * silu[...].astype(F32)).astype(BF16)
    token[...] = jnp.zeros(token.shape, F32)


def finish(slope, silu, grad_act):
    steps = 4
    rows = row_blocks(slope, steps)
    return call(
        finish_kernel,
        (shape(*slope.shape), shape(*slope.shape), shape(8, 128, dtype=F32)),
        (0, 0),
        [rows] * 3,
        (slope, silu, grad_act),
        grid=(steps,),
        out_specs=[rows, rows, fixed(8, 128)],
    )


def dot(left, right, dims):
    product = lax.dot_general(left, right, (dims, ((), ())), preferred_element_type=F32)
    return product.astype(BF16)


def on_device(gate_pre, up_pre, down_weight, grad_out, weight_history, act_history):
    _, feature_place, z = here()
    groups = token_groups()
    swap = [(n, n ^ 1) for n in range(128)]
    weight_q, weight_peak = clip_weight(down_weight, weight_history[None])
    act_q, peaks = activate(gate_pre, up_pre, weight_peak, act_history[None])
    blocks = share(grad_out, peaks, send(peaks, swap))
    blocks = [
        send(block, [(edge[0], edge[1]) for edge in ROUNDS[number]])
        for number, block in enumerate(blocks)
    ]
    grad, peaks = place(blocks)
    weight = stamp(weight_q, peaks)
    before, after = send(weight, feature_ring(1)), send(weight, feature_ring(-1))
    half = weight_q.shape[0] // 2
    weight, peaks = weight_tile(
        weight,
        after,
        send(before[:half], feature_ring(1)),
        send(after[half:], feature_ring(-1)),
        before,
    )
    peaks = jnp.maximum(peaks, send(peaks, swap))
    (act_q,) = gate((act_q,), (grad,))
    act = lax.all_gather(act_q, AXES, axis=0, tiled=True, axis_index_groups=groups)
    slope, silu, token = slopes(gate_pre, up_pre, (grad,))
    before, after = send(grad, hidden_ring(1)), send(grad, hidden_ring(-1))
    half = grad.shape[0] // 2
    tile = grad_tile(
        grad,
        after,
        send(before[:half], hidden_ring(1)),
        send(after[half:], hidden_ring(-1)),
        before,
        (token,),
    )

    def block_of(array, number):
        size = array.shape[1] // N
        return lax.dynamic_slice_in_dim(array, number % N * size, size, axis=1)

    grad_act = dot(tile, weight, ((1,), (1,)))
    grad_act = lax.psum_scatter(
        grad_act, AXES, scatter_dimension=0, tiled=True, axis_index_groups=groups
    )
    far = block_of(weight, z + 2)
    top = send(dot(act[:half], far, ((1,), (0,))), hidden_ring(1))
    bottom = send(dot(act[half:], far, ((1,), (0,))), hidden_ring(-1))
    mixed = [dot(act, block_of(weight, z + step), ((1,), (0,))) for step in (0, 1, 3)]
    (act,) = gate((act,), mixed)
    weight_grad = [
        dot(act, block_of(tile, feature_place + step), ((0,), (0,))) for step in range(N)
    ]
    after, before = add_halves(mixed[1], mixed[2], top, bottom, weight_grad[2:])
    mixed = (mixed[0], send(after, hidden_ring(1)), send(before, hidden_ring(-1)))
    blocks = list(return_blocks(mixed, peaks))
    weight_grad, added = add(ring_exchange(weight_grad, feature_ring), blocks[:1])
    grad_gate, grad_up, finished = finish(slope, silu, grad_act)
    blocks[2:] = gate(blocks[2:], (added,))
    blocks = [
        send(block, [(edge[1], edge[0]) for edge in ROUNDS[number]])
        for number, block in enumerate(blocks)
    ]
    blocks = gate(blocks, (finished,))
    mixed = merge(blocks, ())
    peaks = read_notes(blocks)
    new_weight, new_act = histories(
        peaks, send(peaks, swap), weight_history[None], act_history[None]
    )
    return (mixed, grad_gate, grad_up, weight_grad, new_weight[0], new_act[0])


def solution(mesh):
    cube = Mesh(mesh.devices.reshape(N, N, N, 2), AXES)
    whole = P(("x", "y"), ("z", "c"))
    flipped = P(("z", "c"), ("x", "y"))
    return jax.shard_map(
        on_device,
        mesh=cube,
        in_specs=(whole, whole, flipped, whole, P(), P()),
        out_specs=(whole, whole, whole, flipped, P(), P()),
        check_vma=False,
    )
```

```python
import functools

import jax
import jax.numpy as jnp
import numpy as np
from jax import lax
from jax.experimental import pallas as pl
from jax.experimental.pallas import tpu as pltpu
from jax.sharding import Mesh, PartitionSpec as P

AXES = ("x", "y", "z", "c")
N = 4
BF16 = jnp.bfloat16
F32 = jnp.float32
VMEM_BYTES = 24 * 1024 * 1024
ANYWHERE = pl.BlockSpec(memory_space=pl.ANY)
SCALARS = pl.BlockSpec(memory_space=pltpu.SMEM)
IN_VMEM = pl.BlockSpec(memory_space=pltpu.VMEM)
IN_HBM = pl.BlockSpec(memory_space=pltpu.HBM)
NOTE = 16


def flat(x, y, z, c):
    return ((x % N * N + y % N) * N + z % N) * 2 + c


def places():
    return [(x, y, z, c) for x in range(N) for y in range(N) for z in range(N) for c in range(2)]


def token_ring(step):
    return [
        (flat(x, y, z, c), flat(x, y + step, z, c) if c == 0 else flat(x + step, y, z, c))
        for x, y, z, c in places()
    ]


def feature_ring(step):
    return [
        (flat(x, y, z, c), flat(x + step, y, z, c) if c == 0 else flat(x, y + step, z, c))
        for x, y, z, c in places()
    ]


def hidden_ring(step):
    return [(flat(x, y, z, c), flat(x, y, z + step, c)) for x, y, z, c in places()]


def token_groups():
    first = [[flat(x, y, z, 0) for y in range(N)] for x in range(N) for z in range(N)]
    second = [[flat(x, y, z, 1) for x in range(N)] for y in range(N) for z in range(N)]
    return first + second


def tile_edges():
    edges = []
    for x, y, z, c in places():
        for half in range(2):
            block = 2 * c + half
            edges.append((flat(x, y, z, c), flat(x, block, z, 0), half, y))
            edges.append((flat(x, y, z, c), flat(z, y, block, 1), half, x))
    return edges


def rounds():
    rest = tile_edges()
    out = []
    for _ in range(4):
        outgoing = {}
        for edge in rest:
            outgoing.setdefault(edge[0], []).append(edge)
        chosen = {}

        def augment(owner, seen):
            for edge in outgoing[owner]:
                if edge[1] in seen:
                    continue
                seen.add(edge[1])
                if edge[1] not in chosen or augment(chosen[edge[1]][0], seen):
                    chosen[edge[1]] = edge
                    return True
            return False

        for owner in range(128):
            augment(owner, set())
        picked = sorted(chosen.values())
        out.append(picked)
        rest = [edge for edge in rest if edge not in picked]
    return out


ROUNDS = rounds()
TABLE = np.zeros((8, 128), np.int32)
for number, picked in enumerate(ROUNDS):
    for owner, user, half, slot in picked:
        TABLE[number, owner] = half
        TABLE[4 + number, user] = slot


def send(value, pairs):
    return lax.ppermute(value, AXES, pairs)


def here():
    x, y, z, c = (lax.axis_index(name) for name in AXES)
    return flat(x, y, z, c), jnp.where(c == 0, x, y), z


def call(kernel, out_shape, cost, in_specs, operands, after=(), stored=(), vmem=VMEM_BYTES, **options):
    flops, moved = cost
    count = len(operands)
    extra = len(after) + len(stored)

    def body(*refs):
        kernel(*refs[:count], *refs[count + extra :])

    return pl.pallas_call(
        body,
        out_shape=out_shape,
        in_specs=list(in_specs) + [ANYWHERE] * len(after) + [IN_HBM] * len(stored),
        compiler_params=pltpu.CompilerParams(vmem_limit_bytes=vmem),
        cost_estimate=pl.CostEstimate(flops=flops, bytes_accessed=moved, transcendentals=0),
        **options,
    )(*operands, *after, *stored)


def shape(*dims, dtype=BF16):
    return jax.ShapeDtypeStruct(dims, dtype)


def ring_gather(own, ring):
    far = send(own, ring(2))
    return own, send(own, ring(-1)), far, send(own, ring(1))


def ring_exchange(parts, ring):
    far = send(parts[2], ring(2))
    return parts[0], send(parts[1], ring(1)), far, send(parts[3], ring(-1))


def peak_of(values):
    return jnp.max(jnp.abs(values), axis=0, keepdims=True)


def keep_peak(step, top, peak):
    @pl.when(step == 0)
    def _():
        top[...] = peak

    @pl.when(step > 0)
    def _():
        top[...] = jnp.maximum(top[...], peak)


def row_blocks(array, steps):
    return pl.BlockSpec((array.shape[0] // steps, array.shape[1]), lambda i: (i, 0))


def fixed(*dims):
    return pl.BlockSpec(dims, lambda i: (0, 0))


def note_of(peaks, width):
    row = lax.broadcasted_iota(jnp.int32, (NOTE, width), 0)
    note = jnp.zeros((NOTE, width), F32)
    for number in range(2):
        rest = jnp.broadcast_to(peaks[number : number + 1, :1], (NOTE, width))
        for piece in range(3):
            value = rest.astype(BF16).astype(F32)
            note = jnp.where(row == 3 * number + piece, value, note)
            rest = rest - value
    return note.astype(BF16)


def peaks_in(notes):
    best = []
    for number in range(2):
        values = []
        for note in notes:
            note = note[...].astype(F32)
            pieces = [note[3 * number + piece : 3 * number + piece + 1, :128] for piece in range(3)]
            values.append(pieces[0] + pieces[1] + pieces[2])
        best.append(functools.reduce(jnp.maximum, values))
    row = lax.broadcasted_iota(jnp.int32, (8, 128), 0)
    return jnp.where(row == 0, jnp.broadcast_to(best[0], (8, 128)), jnp.broadcast_to(best[1], (8, 128)))


def note_block(array):
    last = array.shape[0] // NOTE - 1
    return pl.BlockSpec((NOTE, array.shape[1]), lambda *i: (last, 0))


def share_kernel(table, grad, peaks, others, out0, out1, out2, out3):
    me, _, _ = here()
    tokens, width = grad.shape[0], grad.shape[1] // 2
    note = note_of(jnp.maximum(peaks[...], others[...]), width)
    for number, out in enumerate((out0, out1, out2, out3)):
        half = table[number, me]

        @pl.when(half == 0)
        def _():
            out[:tokens, :] = grad[:, :width]

        @pl.when(half == 1)
        def _():
            out[:tokens, :] = grad[:, width:]

        out[tokens:, :] = note


def share(grad, peaks, others):
    block = shape(grad.shape[0] + NOTE, grad.shape[1] // 2)
    return call(
        share_kernel,
        (block, block, block, block),
        (0, 0),
        [SCALARS] + [IN_VMEM] * 3,
        (jnp.asarray(TABLE), grad, peaks, others),
        out_specs=[IN_VMEM] * 4,
    )


def clip_kernel(weight, history, weight_q, peak, top):
    step = pl.program_id(0)
    weight_v = weight[...].astype(F32)
    limit = jnp.max(history[...], axis=1, keepdims=True)
    weight_q[...] = jnp.clip(weight_v, -limit, limit).astype(BF16)
    keep_peak(step, top, peak_of(weight_v))

    @pl.when(step == pl.num_programs(0) - 1)
    def _():
        peak[...] = jnp.broadcast_to(jnp.max(top[...], axis=1, keepdims=True), peak.shape)


def clip_weight(weight, history):
    steps = 2
    rows = row_blocks(weight, steps)
    return call(
        clip_kernel,
        (shape(*weight.shape), shape(8, 128, dtype=F32)),
        (0, 0),
        [rows, fixed(1, history.shape[1])],
        (weight, history),
        grid=(steps,),
        out_specs=[rows, fixed(8, 128)],
        scratch_shapes=[pltpu.VMEM((1, weight.shape[1]), F32)],
    )


def activate_kernel(gate, up, weight_peak, history, act_q, peaks, top):
    step = pl.program_id(0)
    gate_v = gate[...].astype(F32)
    act = gate_v * jax.nn.sigmoid(gate_v) * up[...].astype(F32)
    limit = jnp.max(history[...], axis=1, keepdims=True)
    act_q[...] = jnp.clip(act, -limit, limit).astype(BF16)
    keep_peak(step, top, peak_of(act))

    @pl.when(step == pl.num_programs(0) - 1)
    def _():
        row = lax.broadcasted_iota(jnp.int32, peaks.shape, 0)
        act_peak = jnp.broadcast_to(jnp.max(top[...], axis=1, keepdims=True), peaks.shape)
        peaks[...] = jnp.where(row == 0, act_peak, weight_peak[...])


def activate(gate, up, weight_peak, history):
    steps = 8
    rows = row_blocks(gate, steps)
    return call(
        activate_kernel,
        (shape(*gate.shape), shape(8, 128, dtype=F32)),
        (0, 0),
        [rows, rows, fixed(8, 128), fixed(1, history.shape[1])],
        (gate, up, weight_peak, history),
        grid=(steps,),
        out_specs=[rows, fixed(8, 128)],
        scratch_shapes=[pltpu.VMEM((1, gate.shape[1]), F32)],
    )


def slopes_kernel(gate, up, slope, silu, token):
    gate_v = gate[...].astype(F32)
    sigm = jax.nn.sigmoid(gate_v)
    slope[...] = (up[...].astype(F32) * sigm * (1.0 + gate_v * (1.0 - sigm))).astype(BF16)
    silu[...] = (gate_v * sigm).astype(BF16)
    token[...] = jnp.zeros(token.shape, F32)


def slopes(gate, up, after):
    steps = 8
    rows = row_blocks(gate, steps)
    return call(
        slopes_kernel,
        (shape(*gate.shape), shape(*gate.shape), shape(8, 128, dtype=F32)),
        (0, 0),
        [rows, rows],
        (gate, up),
        after,
        grid=(steps,),
        out_specs=[rows, rows, fixed(8, 128)],
    )


def place_kernel(table, in0, in1, in2, in3, out, peaks):
    me, _, _ = here()
    rows = in0.shape[0] - NOTE
    for number, block in enumerate((in0, in1, in2, in3)):
        start = pl.multiple_of(table[4 + number, me] * rows, rows)
        out[pl.ds(start, rows), :] = block[:rows, :]
    peaks[...] = peaks_in([block[rows:, :] for block in (in0, in1, in2, in3)])


def place(blocks):
    rows, features = blocks[0].shape
    return call(
        place_kernel,
        (shape(4 * (rows - NOTE), features), shape(8, 128, dtype=F32)),
        (0, 0),
        [SCALARS] + [IN_VMEM] * 4,
        (jnp.asarray(TABLE), *blocks),
        out_specs=[IN_VMEM] * 2,
    )


def stamp_kernel(weight, peaks, out):
    rows = weight.shape[0]
    out[:rows, :] = weight[...]
    out[rows:, :] = note_of(peaks[...], weight.shape[1])


def stamp(weight, peaks):
    return call(
        stamp_kernel,
        shape(weight.shape[0] + NOTE, weight.shape[1]),
        (0, 0),
        [IN_VMEM] * 2,
        (weight, peaks),
        out_specs=IN_VMEM,
    )


def gate_kernel(*refs):
    pass


def gate(values, after=(), stored=()):
    count = len(values)
    return call(
        gate_kernel,
        tuple(shape(*value.shape) for value in values),
        (0, 0),
        [ANYWHERE] * count,
        values,
        after,
        stored,
        vmem=1024 * 1024,
        out_specs=[ANYWHERE] * count,
        input_output_aliases={number: number for number in range(count)},
    )


def columns_kernel(place, own, after, far, before, out):
    width = own.shape[1]
    for step, block in enumerate((own, after, far, before)):
        column = (place + step) % N * width
        if not isinstance(column, int):
            column = pl.multiple_of(column, width)
        out[:, pl.ds(column, width)] = block[...]


def half_blocks(steps, dims):
    first = pl.BlockSpec(dims, lambda i: (jnp.minimum(i, steps // 2 - 1), 0))
    second = pl.BlockSpec(dims, lambda i: (jnp.maximum(i - steps // 2, 0), 0))
    return [first, second]


def weight_tile_kernel(own, after, top, bottom, before, note0, note1, note2, note3, out, peaks):
    place = here()[1]
    step = pl.program_id(0)

    @pl.when(step < pl.num_programs(0) // 2)
    def _():
        columns_kernel(place, own, after, top, before, out)

    @pl.when(step >= pl.num_programs(0) // 2)
    def _():
        columns_kernel(place, own, after, bottom, before, out)

    peaks[...] = peaks_in((note0, note1, note2, note3))


def weight_tile(own, after, top, bottom, before):
    steps = 4
    hidden, features = own.shape[0] - NOTE, own.shape[1]
    dims = (hidden // steps, features)
    block = pl.BlockSpec(dims, lambda i: (i, 0))
    out = shape(hidden, N * features)
    noted = (own, after, bottom, before)
    return call(
        weight_tile_kernel,
        (out, shape(8, 128, dtype=F32)),
        (0, 0),
        [block, block, *half_blocks(steps, dims), block] + [note_block(part) for part in noted],
        (own, after, top, bottom, before, *noted),
        grid=(steps,),
        out_specs=[row_blocks(out, steps), fixed(8, 128)],
    )


def raise_kernel(after, before, top, bottom, out_after, out_before):
    rows = top.shape[0]
    out_after[:rows, :] = (after[:rows, :].astype(F32) + top[...].astype(F32)).astype(BF16)
    out_after[rows:, :] = after[rows:, :]
    out_before[:rows, :] = before[:rows, :]
    out_before[rows:, :] = (before[rows:, :].astype(F32) + bottom[...].astype(F32)).astype(BF16)


def add_halves(after, before, top, bottom, order):
    whole = shape(*after.shape)
    return call(
        raise_kernel,
        (whole, whole),
        (0, 0),
        [IN_VMEM] * 4,
        (after, before, top, bottom),
        order,
        out_specs=[IN_VMEM] * 2,
    )


def grad_tile_kernel(own, after, top, bottom, before, out):
    place = here()[2]
    step = pl.program_id(0)

    @pl.when(step < pl.num_programs(0) // 2)
    def _():
        columns_kernel(place, own, after, top, before, out)

    @pl.when(step >= pl.num_programs(0) // 2)
    def _():
        columns_kernel(place, own, after, bottom, before, out)


def grad_tile(own, after, top, bottom, before, order):
    steps = 4
    rows, features = own.shape
    dims = (rows // steps, features)
    block = pl.BlockSpec(dims, lambda i: (i, 0))
    out = shape(rows, N * features)
    return call(
        grad_tile_kernel,
        out,
        (0, 0),
        [block, block, *half_blocks(steps, dims), block],
        (own, after, top, bottom, before),
        order,
        grid=(steps,),
        out_specs=row_blocks(out, steps),
    )


def histories_kernel(peaks, others, old_weight, old_act, new_weight, new_act):
    for row, old, new in ((1, old_weight, new_weight), (0, old_act, new_act)):
        new[:, 1:] = old[:, :-1]
        new[:, :1] = jnp.maximum(peaks[row : row + 1, :1], others[row : row + 1, :1])


def histories(peaks, others, old_weight, old_act):
    new = shape(*old_weight.shape, dtype=F32)
    return call(
        histories_kernel,
        (new, new),
        (0, 0),
        [IN_VMEM] * 4,
        (peaks, others, old_weight, old_act),
        out_specs=[IN_VMEM] * 2,
    )


def return_kernel(table, own, before, after, peaks, out0, out1, out2, out3):
    me, _, _ = here()
    tokens = out0.shape[0] - NOTE
    note = note_of(peaks[...], out0.shape[1])
    for number, out in enumerate((out0, out1, out2, out3)):
        rows = pl.ds(pl.multiple_of(table[4 + number, me] * tokens, tokens), tokens)
        total = own[rows, :].astype(F32) + before[rows, :].astype(F32) + after[rows, :].astype(F32)
        out[:tokens, :] = total.astype(BF16)
        out[tokens:, :] = note


def return_blocks(parts, peaks):
    rows, features = parts[0].shape
    return call(
        return_kernel,
        (shape(rows // N + NOTE, features),) * 4,
        (0, 0),
        [SCALARS] + [IN_VMEM] * 4,
        (jnp.asarray(TABLE), *parts, peaks),
        out_specs=[IN_VMEM] * 4,
    )


def read_kernel(note0, note1, note2, note3, peaks):
    peaks[...] = peaks_in((note0, note1, note2, note3))


def read_notes(blocks):
    return call(
        read_kernel,
        shape(8, 128, dtype=F32),
        (0, 0),
        [note_block(block) for block in blocks],
        blocks,
        grid=(1,),
        out_specs=fixed(8, 128),
    )


def add_kernel(part0, part1, part2, part3, out, token):
    total = part0[...].astype(F32) + part1[...].astype(F32)
    out[...] = (total + (part2[...].astype(F32) + part3[...].astype(F32))).astype(BF16)
    token[...] = jnp.zeros(token.shape, F32)


def add(parts, after):
    steps = 4
    rows = row_blocks(parts[0], steps)
    return call(
        add_kernel,
        (shape(*parts[0].shape), shape(8, 128, dtype=F32)),
        (0, 0),
        [rows] * 4,
        parts,
        after,
        grid=(steps,),
        out_specs=[rows, fixed(8, 128)],
    )


def merge_kernel(table, in0, in1, in2, in3, out):
    me, _, _ = here()
    width = in0.shape[1]
    for half in range(2):
        total = jnp.zeros(in0.shape, F32)
        for number, block in enumerate((in0, in1, in2, in3)):
            keep = (table[number, me] == half).astype(F32)
            total = total + block[...].astype(F32) * keep
        out[:, half * width : (half + 1) * width] = total.astype(BF16)


def merge(blocks, after):
    steps = 2
    tokens, features = blocks[0].shape[0] - NOTE, blocks[0].shape[1]
    block = pl.BlockSpec((tokens // steps, features), lambda i: (i, 0))
    out = shape(tokens, 2 * features)
    return call(
        merge_kernel,
        out,
        (0, 0),
        [SCALARS] + [block] * 4,
        (jnp.asarray(TABLE), *blocks),
        after,
        grid=(steps,),
        out_specs=row_blocks(out, steps),
    )


def finish_kernel(slope, silu, grad_act, grad_gate, grad_up, token):
    value = grad_act[...].astype(F32)
    grad_gate[...] = (value * slope[...].astype(F32)).astype(BF16)
    grad_up[...] = (value * silu[...].astype(F32)).astype(BF16)
    token[...] = jnp.zeros(token.shape, F32)


def finish(slope, silu, grad_act):
    steps = 4
    rows = row_blocks(slope, steps)
    return call(
        finish_kernel,
        (shape(*slope.shape), shape(*slope.shape), shape(8, 128, dtype=F32)),
        (0, 0),
        [rows] * 3,
        (slope, silu, grad_act),
        grid=(steps,),
        out_specs=[rows, rows, fixed(8, 128)],
    )


def dot(left, right, dims):
    product = lax.dot_general(left, right, (dims, ((), ())), preferred_element_type=F32)
    return product.astype(BF16)


def on_device(gate_pre, up_pre, down_weight, grad_out, weight_history, act_history):
    _, feature_place, z = here()
    groups = token_groups()
    swap = [(n, n ^ 1) for n in range(128)]
    weight_q, weight_peak = clip_weight(down_weight, weight_history[None])
    act_q, peaks = activate(gate_pre, up_pre, weight_peak, act_history[None])
    blocks = share(grad_out, peaks, send(peaks, swap))
    blocks = [
        send(block, [(edge[0], edge[1]) for edge in ROUNDS[number]])
        for number, block in enumerate(blocks)
    ]
    grad, peaks = place(blocks)
    weight = stamp(weight_q, peaks)
    before, after = send(weight, feature_ring(1)), send(weight, feature_ring(-1))
    half = weight_q.shape[0] // 2
    weight, peaks = weight_tile(
        weight,
        after,
        send(before[:half], feature_ring(1)),
        send(after[half:], feature_ring(-1)),
        before,
    )
    peaks = jnp.maximum(peaks, send(peaks, swap))
    (act_q,) = gate((act_q,), (grad,))
    act = lax.all_gather(act_q, AXES, axis=0, tiled=True, axis_index_groups=groups)
    slope, silu, token = slopes(gate_pre, up_pre, (grad,))
    before, after = send(grad, hidden_ring(1)), send(grad, hidden_ring(-1))
    half = grad.shape[0] // 2
    tile = grad_tile(
        grad,
        after,
        send(before[:half], hidden_ring(1)),
        send(after[half:], hidden_ring(-1)),
        before,
        (token,),
    )

    def block_of(array, number):
        size = array.shape[1] // N
        return lax.dynamic_slice_in_dim(array, number % N * size, size, axis=1)

    grad_act = dot(tile, weight, ((1,), (1,)))
    grad_act = lax.psum_scatter(
        grad_act, AXES, scatter_dimension=0, tiled=True, axis_index_groups=groups
    )
    far = block_of(weight, z + 2)
    top = send(dot(act[:half], far, ((1,), (0,))), hidden_ring(1))
    bottom = send(dot(act[half:], far, ((1,), (0,))), hidden_ring(-1))
    mixed = [dot(act, block_of(weight, z + step), ((1,), (0,))) for step in (1, 3)]
    (act,) = gate((act,), mixed)
    own = dot(act, block_of(weight, z), ((1,), (0,)))
    weight_grad = [
        dot(act, block_of(tile, feature_place + step), ((0,), (0,))) for step in range(N)
    ]
    after, before = add_halves(*mixed, top, bottom, weight_grad[2:])
    mixed = (own, send(after, hidden_ring(1)), send(before, hidden_ring(-1)))
    blocks = list(return_blocks(mixed, peaks))
    weight_grad, added = add(ring_exchange(weight_grad, feature_ring), blocks[:1])
    grad_gate, grad_up, finished = finish(slope, silu, grad_act)
    blocks[2:] = gate(blocks[2:], (added,))
    blocks = [
        send(block, [(edge[1], edge[0]) for edge in ROUNDS[number]])
        for number, block in enumerate(blocks)
    ]
    blocks = gate(blocks, (finished,))
    mixed = merge(blocks, ())
    peaks = read_notes(blocks)
    new_weight, new_act = histories(
        peaks, send(peaks, swap), weight_history[None], act_history[None]
    )
    return (mixed, grad_gate, grad_up, weight_grad, new_weight[0], new_act[0])


def solution(mesh):
    cube = Mesh(mesh.devices.reshape(N, N, N, 2), AXES)
    whole = P(("x", "y"), ("z", "c"))
    flipped = P(("z", "c"), ("x", "y"))
    return jax.shard_map(
        on_device,
        mesh=cube,
        in_specs=(whole, whole, flipped, whole, P(), P()),
        out_specs=(whole, whole, whole, flipped, P(), P()),
        check_vma=False,
    )
```

```python
import functools

import jax
import jax.numpy as jnp
import numpy as np
from jax import lax
from jax.experimental import pallas as pl
from jax.experimental.pallas import tpu as pltpu
from jax.sharding import Mesh, PartitionSpec as P

AXES = ("x", "y", "z", "c")
N = 4
BF16 = jnp.bfloat16
F32 = jnp.float32
VMEM_BYTES = 24 * 1024 * 1024
ANYWHERE = pl.BlockSpec(memory_space=pl.ANY)
SCALARS = pl.BlockSpec(memory_space=pltpu.SMEM)
IN_VMEM = pl.BlockSpec(memory_space=pltpu.VMEM)
IN_HBM = pl.BlockSpec(memory_space=pltpu.HBM)
NOTE = 16


def flat(x, y, z, c):
    return ((x % N * N + y % N) * N + z % N) * 2 + c


def places():
    return [(x, y, z, c) for x in range(N) for y in range(N) for z in range(N) for c in range(2)]


def token_ring(step):
    return [
        (flat(x, y, z, c), flat(x, y + step, z, c) if c == 0 else flat(x + step, y, z, c))
        for x, y, z, c in places()
    ]


def feature_ring(step):
    return [
        (flat(x, y, z, c), flat(x + step, y, z, c) if c == 0 else flat(x, y + step, z, c))
        for x, y, z, c in places()
    ]


def hidden_ring(step):
    return [(flat(x, y, z, c), flat(x, y, z + step, c)) for x, y, z, c in places()]


def token_groups():
    first = [[flat(x, y, z, 0) for y in range(N)] for x in range(N) for z in range(N)]
    second = [[flat(x, y, z, 1) for x in range(N)] for y in range(N) for z in range(N)]
    return first + second


def tile_edges():
    edges = []
    for x, y, z, c in places():
        for half in range(2):
            block = 2 * c + half
            edges.append((flat(x, y, z, c), flat(x, block, z, 0), half, y))
            edges.append((flat(x, y, z, c), flat(z, y, block, 1), half, x))
    return edges


def rounds():
    rest = tile_edges()
    out = []
    for _ in range(4):
        outgoing = {}
        for edge in rest:
            outgoing.setdefault(edge[0], []).append(edge)
        chosen = {}

        def augment(owner, seen):
            for edge in outgoing[owner]:
                if edge[1] in seen:
                    continue
                seen.add(edge[1])
                if edge[1] not in chosen or augment(chosen[edge[1]][0], seen):
                    chosen[edge[1]] = edge
                    return True
            return False

        for owner in range(128):
            augment(owner, set())
        picked = sorted(chosen.values())
        out.append(picked)
        rest = [edge for edge in rest if edge not in picked]
    return out


ROUNDS = rounds()
TABLE = np.zeros((8, 128), np.int32)
for number, picked in enumerate(ROUNDS):
    for owner, user, half, slot in picked:
        TABLE[number, owner] = half
        TABLE[4 + number, user] = slot


def send(value, pairs):
    return lax.ppermute(value, AXES, pairs)


def here():
    x, y, z, c = (lax.axis_index(name) for name in AXES)
    return flat(x, y, z, c), jnp.where(c == 0, x, y), z


def call(kernel, out_shape, cost, in_specs, operands, after=(), stored=(), vmem=VMEM_BYTES, **options):
    flops, moved = cost
    count = len(operands)
    extra = len(after) + len(stored)

    def body(*refs):
        kernel(*refs[:count], *refs[count + extra :])

    return pl.pallas_call(
        body,
        out_shape=out_shape,
        in_specs=list(in_specs) + [ANYWHERE] * len(after) + [IN_HBM] * len(stored),
        compiler_params=pltpu.CompilerParams(vmem_limit_bytes=vmem),
        cost_estimate=pl.CostEstimate(flops=flops, bytes_accessed=moved, transcendentals=0),
        **options,
    )(*operands, *after, *stored)


def shape(*dims, dtype=BF16):
    return jax.ShapeDtypeStruct(dims, dtype)


def ring_gather(own, ring):
    far = send(own, ring(2))
    return own, send(own, ring(-1)), far, send(own, ring(1))


def ring_exchange(parts, ring):
    far = send(parts[2], ring(2))
    return parts[0], send(parts[1], ring(1)), far, send(parts[3], ring(-1))


def peak_of(values):
    return jnp.max(jnp.abs(values), axis=0, keepdims=True)


def keep_peak(step, top, peak):
    @pl.when(step == 0)
    def _():
        top[...] = peak

    @pl.when(step > 0)
    def _():
        top[...] = jnp.maximum(top[...], peak)


def row_blocks(array, steps):
    return pl.BlockSpec((array.shape[0] // steps, array.shape[1]), lambda i: (i, 0))


def fixed(*dims):
    return pl.BlockSpec(dims, lambda i: (0, 0))


def note_of(peaks, width):
    row = lax.broadcasted_iota(jnp.int32, (NOTE, width), 0)
    note = jnp.zeros((NOTE, width), F32)
    for number in range(2):
        rest = jnp.broadcast_to(peaks[number : number + 1, :1], (NOTE, width))
        for piece in range(3):
            value = rest.astype(BF16).astype(F32)
            note = jnp.where(row == 3 * number + piece, value, note)
            rest = rest - value
    return note.astype(BF16)


def peaks_in(notes):
    best = []
    for number in range(2):
        values = []
        for note in notes:
            note = note[...].astype(F32)
            pieces = [note[3 * number + piece : 3 * number + piece + 1, :128] for piece in range(3)]
            values.append(pieces[0] + pieces[1] + pieces[2])
        best.append(functools.reduce(jnp.maximum, values))
    row = lax.broadcasted_iota(jnp.int32, (8, 128), 0)
    return jnp.where(row == 0, jnp.broadcast_to(best[0], (8, 128)), jnp.broadcast_to(best[1], (8, 128)))


def note_block(array):
    last = array.shape[0] // NOTE - 1
    return pl.BlockSpec((NOTE, array.shape[1]), lambda *i: (last, 0))


def share_kernel(table, grad, peaks, others, out0, out1, out2, out3):
    me, _, _ = here()
    tokens, width = grad.shape[0], grad.shape[1] // 2
    note = note_of(jnp.maximum(peaks[...], others[...]), width)
    for number, out in enumerate((out0, out1, out2, out3)):
        half = table[number, me]

        @pl.when(half == 0)
        def _():
            out[:tokens, :] = grad[:, :width]

        @pl.when(half == 1)
        def _():
            out[:tokens, :] = grad[:, width:]

        out[tokens:, :] = note


def share(grad, peaks, others):
    block = shape(grad.shape[0] + NOTE, grad.shape[1] // 2)
    return call(
        share_kernel,
        (block, block, block, block),
        (0, 0),
        [SCALARS] + [IN_VMEM] * 3,
        (jnp.asarray(TABLE), grad, peaks, others),
        out_specs=[IN_VMEM] * 4,
    )


def clip_kernel(weight, history, weight_q, peak, top):
    step = pl.program_id(0)
    weight_v = weight[...].astype(F32)
    limit = jnp.max(history[...], axis=1, keepdims=True)
    weight_q[...] = jnp.clip(weight_v, -limit, limit).astype(BF16)
    keep_peak(step, top, peak_of(weight_v))

    @pl.when(step == pl.num_programs(0) - 1)
    def _():
        peak[...] = jnp.broadcast_to(jnp.max(top[...], axis=1, keepdims=True), peak.shape)


def clip_weight(weight, history):
    steps = 2
    rows = row_blocks(weight, steps)
    return call(
        clip_kernel,
        (shape(*weight.shape), shape(8, 128, dtype=F32)),
        (0, 0),
        [rows, fixed(1, history.shape[1])],
        (weight, history),
        grid=(steps,),
        out_specs=[rows, fixed(8, 128)],
        scratch_shapes=[pltpu.VMEM((1, weight.shape[1]), F32)],
    )


def activate_kernel(gate, up, weight_peak, history, act_q, peaks, top):
    step = pl.program_id(0)
    gate_v = gate[...].astype(F32)
    act = gate_v * jax.nn.sigmoid(gate_v) * up[...].astype(F32)
    limit = jnp.max(history[...], axis=1, keepdims=True)
    act_q[...] = jnp.clip(act, -limit, limit).astype(BF16)
    keep_peak(step, top, peak_of(act))

    @pl.when(step == pl.num_programs(0) - 1)
    def _():
        row = lax.broadcasted_iota(jnp.int32, peaks.shape, 0)
        act_peak = jnp.broadcast_to(jnp.max(top[...], axis=1, keepdims=True), peaks.shape)
        peaks[...] = jnp.where(row == 0, act_peak, weight_peak[...])


def activate(gate, up, weight_peak, history):
    steps = 8
    rows = row_blocks(gate, steps)
    return call(
        activate_kernel,
        (shape(*gate.shape), shape(8, 128, dtype=F32)),
        (0, 0),
        [rows, rows, fixed(8, 128), fixed(1, history.shape[1])],
        (gate, up, weight_peak, history),
        grid=(steps,),
        out_specs=[rows, fixed(8, 128)],
        scratch_shapes=[pltpu.VMEM((1, gate.shape[1]), F32)],
    )


def slopes_kernel(gate, up, slope, silu, token):
    gate_v = gate[...].astype(F32)
    sigm = jax.nn.sigmoid(gate_v)
    slope[...] = (up[...].astype(F32) * sigm * (1.0 + gate_v * (1.0 - sigm))).astype(BF16)
    silu[...] = (gate_v * sigm).astype(BF16)
    token[...] = jnp.zeros(token.shape, F32)


def slopes(gate, up, after):
    steps = 8
    rows = row_blocks(gate, steps)
    return call(
        slopes_kernel,
        (shape(*gate.shape), shape(*gate.shape), shape(8, 128, dtype=F32)),
        (0, 0),
        [rows, rows],
        (gate, up),
        after,
        grid=(steps,),
        out_specs=[rows, rows, fixed(8, 128)],
    )


def place_kernel(table, in0, in1, in2, in3, out, peaks):
    me, _, _ = here()
    rows = in0.shape[0] - NOTE
    for number, block in enumerate((in0, in1, in2, in3)):
        start = pl.multiple_of(table[4 + number, me] * rows, rows)
        out[pl.ds(start, rows), :] = block[:rows, :]
    peaks[...] = peaks_in([block[rows:, :] for block in (in0, in1, in2, in3)])


def place(blocks):
    rows, features = blocks[0].shape
    return call(
        place_kernel,
        (shape(4 * (rows - NOTE), features), shape(8, 128, dtype=F32)),
        (0, 0),
        [SCALARS] + [IN_VMEM] * 4,
        (jnp.asarray(TABLE), *blocks),
        out_specs=[IN_VMEM] * 2,
    )


def stamp_kernel(weight, peaks, out):
    rows = weight.shape[0]
    out[:rows, :] = weight[...]
    out[rows:, :] = note_of(peaks[...], weight.shape[1])


def stamp(weight, peaks):
    return call(
        stamp_kernel,
        shape(weight.shape[0] + NOTE, weight.shape[1]),
        (0, 0),
        [IN_VMEM] * 2,
        (weight, peaks),
        out_specs=IN_VMEM,
    )


def gate_kernel(*refs):
    pass


def gate(values, after=(), stored=()):
    count = len(values)
    return call(
        gate_kernel,
        tuple(shape(*value.shape) for value in values),
        (0, 0),
        [ANYWHERE] * count,
        values,
        after,
        stored,
        vmem=1024 * 1024,
        out_specs=[ANYWHERE] * count,
        input_output_aliases={number: number for number in range(count)},
    )


def columns_kernel(place, own, after, far, before, out):
    width = own.shape[1]
    for step, block in enumerate((own, after, far, before)):
        column = (place + step) % N * width
        if not isinstance(column, int):
            column = pl.multiple_of(column, width)
        out[:, pl.ds(column, width)] = block[...]


def half_blocks(steps, dims):
    first = pl.BlockSpec(dims, lambda i: (jnp.minimum(i, steps // 2 - 1), 0))
    second = pl.BlockSpec(dims, lambda i: (jnp.maximum(i - steps // 2, 0), 0))
    return [first, second]


def weight_tile_kernel(own, after, top, bottom, before, note0, note1, note2, note3, out, peaks):
    place = here()[1]
    step = pl.program_id(0)

    @pl.when(step < pl.num_programs(0) // 2)
    def _():
        columns_kernel(place, own, after, top, before, out)

    @pl.when(step >= pl.num_programs(0) // 2)
    def _():
        columns_kernel(place, own, after, bottom, before, out)

    peaks[...] = peaks_in((note0, note1, note2, note3))


def weight_tile(own, after, top, bottom, before):
    steps = 4
    hidden, features = own.shape[0] - NOTE, own.shape[1]
    dims = (hidden // steps, features)
    block = pl.BlockSpec(dims, lambda i: (i, 0))
    out = shape(hidden, N * features)
    noted = (own, after, bottom, before)
    return call(
        weight_tile_kernel,
        (out, shape(8, 128, dtype=F32)),
        (0, 0),
        [block, block, *half_blocks(steps, dims), block] + [note_block(part) for part in noted],
        (own, after, top, bottom, before, *noted),
        grid=(steps,),
        out_specs=[row_blocks(out, steps), fixed(8, 128)],
    )


def raise_kernel(after, before, top, bottom, out_after, out_before):
    rows = top.shape[0]
    out_after[:rows, :] = (after[:rows, :].astype(F32) + top[...].astype(F32)).astype(BF16)
    out_after[rows:, :] = after[rows:, :]
    out_before[:rows, :] = before[:rows, :]
    out_before[rows:, :] = (before[rows:, :].astype(F32) + bottom[...].astype(F32)).astype(BF16)


def add_halves(after, before, top, bottom, order):
    whole = shape(*after.shape)
    return call(
        raise_kernel,
        (whole, whole),
        (0, 0),
        [IN_VMEM] * 4,
        (after, before, top, bottom),
        order,
        out_specs=[IN_VMEM] * 2,
    )


def grad_tile_kernel(own, after, top, bottom, before, out):
    place = here()[2]
    step = pl.program_id(0)

    @pl.when(step < pl.num_programs(0) // 2)
    def _():
        columns_kernel(place, own, after, top, before, out)

    @pl.when(step >= pl.num_programs(0) // 2)
    def _():
        columns_kernel(place, own, after, bottom, before, out)


def grad_tile(own, after, top, bottom, before, order):
    steps = 4
    rows, features = own.shape
    dims = (rows // steps, features)
    block = pl.BlockSpec(dims, lambda i: (i, 0))
    out = shape(rows, N * features)
    return call(
        grad_tile_kernel,
        out,
        (0, 0),
        [block, block, *half_blocks(steps, dims), block],
        (own, after, top, bottom, before),
        order,
        grid=(steps,),
        out_specs=row_blocks(out, steps),
    )


def histories_kernel(peaks, others, old_weight, old_act, new_weight, new_act):
    for row, old, new in ((1, old_weight, new_weight), (0, old_act, new_act)):
        new[:, 1:] = old[:, :-1]
        new[:, :1] = jnp.maximum(peaks[row : row + 1, :1], others[row : row + 1, :1])


def histories(peaks, others, old_weight, old_act):
    new = shape(*old_weight.shape, dtype=F32)
    return call(
        histories_kernel,
        (new, new),
        (0, 0),
        [IN_VMEM] * 4,
        (peaks, others, old_weight, old_act),
        out_specs=[IN_VMEM] * 2,
    )


def return_kernel(table, own, before, after, peaks, out0, out1, out2, out3):
    me, _, _ = here()
    tokens = out0.shape[0] - NOTE
    note = note_of(peaks[...], out0.shape[1])
    for number, out in enumerate((out0, out1, out2, out3)):
        rows = pl.ds(pl.multiple_of(table[4 + number, me] * tokens, tokens), tokens)
        total = own[rows, :].astype(F32) + before[rows, :].astype(F32) + after[rows, :].astype(F32)
        out[:tokens, :] = total.astype(BF16)
        out[tokens:, :] = note


def return_blocks(parts, peaks, after):
    rows, features = parts[0].shape
    return call(
        return_kernel,
        (shape(rows // N + NOTE, features),) * 4,
        (0, 0),
        [SCALARS] + [IN_VMEM] * 4,
        (jnp.asarray(TABLE), *parts, peaks),
        after,
        out_specs=[IN_VMEM] * 4,
    )


def read_kernel(note0, note1, note2, note3, peaks):
    peaks[...] = peaks_in((note0, note1, note2, note3))


def read_notes(blocks):
    return call(
        read_kernel,
        shape(8, 128, dtype=F32),
        (0, 0),
        [note_block(block) for block in blocks],
        blocks,
        grid=(1,),
        out_specs=fixed(8, 128),
    )


def add_kernel(part0, part1, part2, part3, out, token):
    total = part0[...].astype(F32) + part1[...].astype(F32)
    out[...] = (total + (part2[...].astype(F32) + part3[...].astype(F32))).astype(BF16)
    token[...] = jnp.zeros(token.shape, F32)


def add(parts, after):
    steps = 4
    rows = row_blocks(parts[0], steps)
    return call(
        add_kernel,
        (shape(*parts[0].shape), shape(8, 128, dtype=F32)),
        (0, 0),
        [rows] * 4,
        parts,
        after,
        grid=(steps,),
        out_specs=[rows, fixed(8, 128)],
    )


def merge_kernel(table, in0, in1, in2, in3, out):
    me, _, _ = here()
    width = in0.shape[1]
    for half in range(2):
        total = jnp.zeros(in0.shape, F32)
        for number, block in enumerate((in0, in1, in2, in3)):
            keep = (table[number, me] == half).astype(F32)
            total = total + block[...].astype(F32) * keep
        out[:, half * width : (half + 1) * width] = total.astype(BF16)


def merge(blocks, after):
    steps = 2
    tokens, features = blocks[0].shape[0] - NOTE, blocks[0].shape[1]
    block = pl.BlockSpec((tokens // steps, features), lambda i: (i, 0))
    out = shape(tokens, 2 * features)
    return call(
        merge_kernel,
        out,
        (0, 0),
        [SCALARS] + [block] * 4,
        (jnp.asarray(TABLE), *blocks),
        after,
        grid=(steps,),
        out_specs=row_blocks(out, steps),
    )


def finish_kernel(slope, silu, grad_act, grad_gate, grad_up, token):
    value = grad_act[...].astype(F32)
    grad_gate[...] = (value * slope[...].astype(F32)).astype(BF16)
    grad_up[...] = (value * silu[...].astype(F32)).astype(BF16)
    token[...] = jnp.zeros(token.shape, F32)


def finish(slope, silu, grad_act):
    steps = 4
    rows = row_blocks(slope, steps)
    return call(
        finish_kernel,
        (shape(*slope.shape), shape(*slope.shape), shape(8, 128, dtype=F32)),
        (0, 0),
        [rows] * 3,
        (slope, silu, grad_act),
        grid=(steps,),
        out_specs=[rows, rows, fixed(8, 128)],
    )


def dot(left, right, dims):
    product = lax.dot_general(left, right, (dims, ((), ())), preferred_element_type=F32)
    return product.astype(BF16)


def on_device(gate_pre, up_pre, down_weight, grad_out, weight_history, act_history):
    _, feature_place, z = here()
    groups = token_groups()
    swap = [(n, n ^ 1) for n in range(128)]
    weight_q, weight_peak = clip_weight(down_weight, weight_history[None])
    act_q, peaks = activate(gate_pre, up_pre, weight_peak, act_history[None])
    blocks = share(grad_out, peaks, send(peaks, swap))
    blocks = [
        send(block, [(edge[0], edge[1]) for edge in ROUNDS[number]])
        for number, block in enumerate(blocks)
    ]
    grad, peaks = place(blocks)
    weight = stamp(weight_q, peaks)
    before, after = send(weight, feature_ring(1)), send(weight, feature_ring(-1))
    half = weight_q.shape[0] // 2
    weight, peaks = weight_tile(
        weight,
        after,
        send(before[:half], feature_ring(1)),
        send(after[half:], feature_ring(-1)),
        before,
    )
    peaks = jnp.maximum(peaks, send(peaks, swap))
    (act_q,) = gate((act_q,), (grad,))
    act = lax.all_gather(act_q, AXES, axis=0, tiled=True, axis_index_groups=groups)
    slope, silu, token = slopes(gate_pre, up_pre, (grad,))
    before, after = send(grad, hidden_ring(1)), send(grad, hidden_ring(-1))
    half = grad.shape[0] // 2
    tile = grad_tile(
        grad,
        after,
        send(before[:half], hidden_ring(1)),
        send(after[half:], hidden_ring(-1)),
        before,
        (token,),
    )

    def block_of(array, number):
        size = array.shape[1] // N
        return lax.dynamic_slice_in_dim(array, number % N * size, size, axis=1)

    grad_act = dot(tile, weight, ((1,), (1,)))
    grad_act = lax.psum_scatter(
        grad_act, AXES, scatter_dimension=0, tiled=True, axis_index_groups=groups
    )
    far = block_of(weight, z + 2)
    top = send(dot(act[:half], far, ((1,), (0,))), hidden_ring(1))
    bottom = send(dot(act[half:], far, ((1,), (0,))), hidden_ring(-1))
    mixed = [dot(act, block_of(weight, z + step), ((1,), (0,))) for step in (1, 3)]
    (act,) = gate((act,), mixed)
    own = dot(act, block_of(weight, z), ((1,), (0,)))
    weight_grad = [
        dot(act, block_of(tile, feature_place + step), ((0,), (0,))) for step in range(N)
    ]
    after, before = add_halves(*mixed, top, bottom, weight_grad[2:])
    mixed = (own, send(after, hidden_ring(1)), send(before, hidden_ring(-1)))
    blocks = list(return_blocks(mixed, peaks, weight_grad[:1]))
    parts = ring_exchange(weight_grad, feature_ring)
    blocks[2:] = gate(blocks[2:], (*parts[1:], blocks[0]))
    grad_gate, grad_up, finished = finish(slope, silu, grad_act)
    weight_grad, added = add(parts, blocks[2:])
    blocks = [
        send(block, [(edge[1], edge[0]) for edge in ROUNDS[number]])
        for number, block in enumerate(blocks)
    ]
    blocks = gate(blocks, (added, finished))
    mixed = merge(blocks, ())
    peaks = read_notes(blocks)
    new_weight, new_act = histories(
        peaks, send(peaks, swap), weight_history[None], act_history[None]
    )
    return (mixed, grad_gate, grad_up, weight_grad, new_weight[0], new_act[0])


def solution(mesh):
    cube = Mesh(mesh.devices.reshape(N, N, N, 2), AXES)
    whole = P(("x", "y"), ("z", "c"))
    flipped = P(("z", "c"), ("x", "y"))
    return jax.shard_map(
        on_device,
        mesh=cube,
        in_specs=(whole, whole, flipped, whole, P(), P()),
        out_specs=(whole, whole, whole, flipped, P(), P()),
        check_vma=False,
    )
```
